256 devices in a mesh: pairs: 64 (over x_lo, y, z), chan: 4 (over x_hi, core).
Axes of the slice: x: 4 (x_hi: 2, x_lo: 2; x = x_hi * 2 + x_lo), y: 4, z: 8, core: 2. Of those that a mesh axis runs over, the one named last changes fastest.
Arguments:
- coherency: bfloat16 [64, 8, 16, 2, 8, 256], P('pairs', None, 'chan'), may hold values from -6 to 6
- visibility: bfloat16 [64, 16, 2, 8, 256], P('pairs', 'chan'), may hold values from -6 to 6
- tile_map: int32 [64, 2], P('pairs'), may hold values from 0 to 31, as said below
- flag_mask: int32 [64, 256], P('pairs'), may hold values from 0 to 1, as said below
- gains_start: float32 [8, 16, 8, 512], P(None, 'chan', None, 'pairs'), may hold values from -1 to 2
- penalty: float32 [8], replicated, may hold values from 100 to 3000
Outputs:
- solved_gains: float32 [8, 16, 8, 512], P(None, 'chan', None, 'pairs')
- residual: bfloat16 [64, 16, 2, 8, 256], P('pairs', 'chan')
The draws below stay inside these ranges and needn't reach their ends.
Inputs may be any that keep to these rules, and one draw needn't show every extreme that they name: `tile_map`: each row names blocks a <= b of an upper tile; no upper tile is named by two slots with used pairs. `flag_mask`: 1 only at pairs of a distinct upper tile, and in a diagonal tile only where i < j.
All inputs are finite; a program needn't handle non-finite values.
Results may differ from the reference program's by a relative error of at most 0.001.
Values sent between devices are 32-bit elements; how exact they have to be, the bound alone decides.
No kernel may reach another device: no remote copies, remote signals or barrier semaphores. Data moves between devices by JAX's collectives and lax.ppermute only.
A program may use at most 128 MiB of HBM per device.

```python
import math
import jax
import jax.numpy as jnp
from jax import lax

S = 512
K = 8
F = 16
T_SIZE = 2
P_SIZE = 3
ITERS = 3
SB = 16
TILES = 64


def slot_tiles(key):
    blocks = S // SB
    upper = blocks * (blocks + 1) // 2
    count = max(TILES, upper)
    order = jax.random.permutation(key, count)[:TILES].astype(jnp.int32)
    live = order < upper
    index = jnp.where(live, order, 0)
    rows = jnp.arange(blocks, dtype=jnp.int32)
    offsets = rows * blocks - rows * (rows - 1) // 2
    first = jnp.sum((offsets[None, 1:] <= index[:, None]).astype(jnp.int32), axis=1)
    second = first + index - jnp.take(offsets, first)
    spare = order % blocks
    first = jnp.where(live, first, spare)
    second = jnp.where(live, second, spare)
    return (first, second, live)


def draw_tile_map(key, part):
    first, second, live = slot_tiles(key)
    return jnp.stack([first, second], 1).astype(jnp.int32)


def draw_flag_mask(key, part):
    first, second, live = slot_tiles(key)
    key = jax.random.fold_in(key, 5)
    level_key, keep_key = jax.random.split(key)
    level = jax.random.randint(level_key, (TILES,), 0, 6)
    keep = jax.random.randint(keep_key, (TILES, SB * SB), 0, 8) >= level[:, None]
    slots = jnp.arange(SB * SB, dtype=jnp.int32)
    upper_pair = slots // SB < slots % SB
    upper = (first < second)[:, None] | upper_pair[None, :]
    return (live[:, None] & upper & keep).astype(jnp.int32)


def draw_gains_start(key, part):
    key = jax.random.fold_in(key, 7)
    noise = jnp.clip(0.3 * jax.random.normal(key, (K, F, 8, S), jnp.float32), -1.0, 1.0)
    component = jax.lax.broadcasted_iota(jnp.int32, (K, F, 8, S), 2)
    identity = jnp.where((component == 0) | (component == 3), 1.0, 0.0)
    return (identity + noise).astype(jnp.float32)


def level_of(rng, extent, cuts, low, high):
    loudness, own = 1.0, jax.random.fold_in(rng, 6)
    for axis_at, parts in cuts:
        draws = jnp.exp(jax.random.uniform(jax.random.fold_in(own, axis_at), (parts,), jnp.float32, low / len(cuts), high / len(cuts)))
        loudness = loudness * jnp.repeat(draws, extent[axis_at] // parts).reshape([-1 if axis == axis_at else 1 for axis in range(len(extent))])
    return loudness


def scatter_about(rng, shape, scale, reach, cuts=(), held_as=jnp.bfloat16):
    level = level_of(rng, shape, cuts, -0.22, 0.18) if cuts else 1.0
    drawn = jax.random.normal(rng, shape, jnp.float32) * scale * level
    return jnp.minimum(jnp.maximum(drawn, -reach), reach).astype(held_as)


def setup_inputs(seed: int = 0) -> dict:
    splits = jax.random.split(jax.random.key(seed), 7)
    coherency = scatter_about(splits[0], (TILES, K, F, T_SIZE, 8, SB * SB), 1.0, 6.0, ((0, 64), (2, 4)))
    visibility = scatter_about(splits[1], (TILES, F, T_SIZE, 8, SB * SB), 1.0, 6.0, ((0, 64), (1, 4)))
    tile_map = draw_tile_map(jax.random.fold_in(splits[6], 71), 0)
    flag_mask = draw_flag_mask(jax.random.fold_in(splits[6], 71), 0)
    gains_start = draw_gains_start(jax.random.fold_in(splits[6], 71), 0)
    penalty = jnp.clip(jnp.exp(jax.random.uniform(splits[5], (K,), jnp.float32, math.log(100.0), math.log(3000.0))), 100.0, 3000.0)
    return dict(coherency=coherency, visibility=visibility, tile_map=tile_map, flag_mask=flag_mask, gains_start=gains_start, penalty=penalty)


def split_parts(matrix):
    shape = matrix.shape
    blocks = matrix.reshape(shape[:-2] + (2, 2, 2, shape[-1]))
    return (blocks[..., 0, :, :, :], blocks[..., 1, :, :, :])

def join_parts(real, imag):
    shape = real.shape
    return jnp.stack([real, imag], -4).reshape(shape[:-3] + (8, shape[-1]))

def complex_product(left, right):
    entries_re = []
    entries_im = []
    for row in range(2):
        for col in range(2):
            real = None
            imag = None
            for inner in range(2):
                l_re = left[..., 2 * row + inner, :]
                l_im = left[..., 4 + 2 * row + inner, :]
                r_re = right[..., 2 * inner + col, :]
                r_im = right[..., 4 + 2 * inner + col, :]
                term_re = l_re * r_re - l_im * r_im
                term_im = l_re * r_im + l_im * r_re
                real = term_re if real is None else real + term_re
                imag = term_im if imag is None else imag + term_im
            entries_re.append(real)
            entries_im.append(imag)
    return jnp.stack(entries_re + entries_im, -2)

def conj_trans(matrix):
    picks = [matrix[..., index, :] for index in (0, 2, 1, 3)]
    negs = [-matrix[..., index, :] for index in (4, 6, 5, 7)]
    return jnp.stack(picks + negs, -2)

def poly_table(count, terms):
    points = (2.0 * jnp.arange(count, dtype=jnp.float32) + 1.0) / count - 1.0
    columns = []
    for power in range(terms):
        vector = points ** power
        for column in columns:
            vector = vector - jnp.sum(column * vector) * column
        vector = vector / jnp.sqrt(jnp.sum(vector * vector))
        columns.append(vector)
    return jnp.stack(columns, 1)

def fit_channels(table, gains):
    coef = jnp.einsum('fm,kfcs->kmcs', table, gains, precision=lax.Precision.HIGHEST)
    return jnp.einsum('fm,kmcs->kfcs', table, coef, precision=lax.Precision.HIGHEST)

def pair_gains(block_a, block_b):
    width = block_a.shape[-1]
    rows_p = jnp.broadcast_to(block_a[..., :, None], block_a.shape + (width,))
    rows_q = jnp.broadcast_to(block_b[..., None, :], block_b.shape + (width,))
    rows_p = rows_p.reshape(block_a.shape[:-1] + (width * width,))
    rows_q = rows_q.reshape(block_b.shape[:-1] + (width * width,))
    return (jnp.expand_dims(rows_p, -3), jnp.expand_dims(rows_q, -3))

def normal_terms(coherency, visibility, flag_row, rows_p, rows_q):
    model_in = coherency.astype(jnp.float32)
    observed = visibility.astype(jnp.float32)
    right_z = complex_product(model_in, conj_trans(rows_q))
    model = complex_product(rows_p, right_z)
    resid = observed - lax.optimization_barrier(jnp.sum(model, axis=-5))
    target = jnp.expand_dims(resid, -5) + model
    left_w = complex_product(rows_p, model_in)
    weight = flag_row.astype(jnp.float32)[..., None, None, None, None, :]
    side_p = jnp.concatenate([complex_product(target, conj_trans(right_z)), complex_product(right_z, conj_trans(right_z))], -2)
    side_q = jnp.concatenate([complex_product(conj_trans(target), left_w), complex_product(conj_trans(left_w), left_w)], -2)
    side_p = lax.optimization_barrier(jnp.sum(weight * side_p, axis=-3))
    side_q = lax.optimization_barrier(jnp.sum(weight * side_q, axis=-3))
    side_p = side_p.reshape(side_p.shape[:-1] + (SB, SB)).sum(-1)
    side_q = side_q.reshape(side_q.shape[:-1] + (SB, SB)).sum(-2)
    return (side_p, side_q)

def update_gains(normal, consensus, penalty):
    numer = normal[:, :, :8, :]
    denom = normal[:, :, 8:, :]
    weight_four = penalty.reshape(-1, 1, 1, 1)
    weight_three = penalty.reshape(-1, 1, 1)
    target = numer + weight_four * consensus
    den_re, den_im = split_parts(denom)
    diag_first = den_re[..., 0, 0, :] + weight_three
    diag_second = den_re[..., 1, 1, :] + weight_three
    off_re = 0.5 * (den_re[..., 0, 1, :] + den_re[..., 1, 0, :])
    off_im = 0.5 * (den_im[..., 0, 1, :] - den_im[..., 1, 0, :])
    determinant = diag_first * diag_second - off_re * off_re - off_im * off_im
    zeros = jnp.zeros_like(off_re)
    scale = determinant[..., None, None, :]
    inverse_re = jnp.stack([jnp.stack([diag_second, -off_re], -2), jnp.stack([-off_re, diag_first], -2)], -3) / scale
    inverse_im = jnp.stack([jnp.stack([zeros, -off_im], -2), jnp.stack([off_im, zeros], -2)], -3) / scale
    return complex_product(target, join_parts(inverse_re, inverse_im))

def block_gains(gains, block):
    return lax.dynamic_slice_in_dim(gains, (block * SB).astype(jnp.int32), SB, 3)

def add_block(carry, piece, block):
    start = (block * SB).astype(jnp.int32)
    current = lax.dynamic_slice_in_dim(carry, start, SB, 3)
    return lax.dynamic_update_slice_in_dim(carry, current + piece, start, 3)

def gather_normals(coherency, visibility, tile_map, flag_mask, gains):

    def step(carry, item):
        model_in, observed, pair, flag_row = item
        rows_p, rows_q = pair_gains(block_gains(gains, pair[0]), block_gains(gains, pair[1]))
        side_p, side_q = normal_terms(model_in, observed, flag_row, rows_p, rows_q)
        carry = add_block(carry, side_p, pair[0])
        carry = add_block(carry, side_q, pair[1])
        return (carry, None)
    start = jnp.zeros((K, F, 16, S), jnp.float32)
    total, unused = lax.scan(step, start, (coherency, visibility, tile_map, flag_mask))
    return total

def reference(coherency, visibility, tile_map, flag_mask, gains_start, penalty):
    table = poly_table(F, P_SIZE)
    gains = gains_start
    consensus = fit_channels(table, gains)
    for sweep in range(ITERS):
        normal = gather_normals(coherency, visibility, tile_map, flag_mask, gains)
        gains = update_gains(normal, consensus, penalty)
        if sweep + 1 < ITERS:
            consensus = fit_channels(table, gains)

    def tile_residual(item):
        model_in, observed, pair = item
        rows_p, rows_q = pair_gains(block_gains(gains, pair[0]), block_gains(gains, pair[1]))
        model = complex_product(rows_p, complex_product(model_in.astype(jnp.float32), conj_trans(rows_q)))
        return (observed.astype(jnp.float32) - lax.optimization_barrier(jnp.sum(model, axis=-5))).astype(jnp.bfloat16)
    residual = lax.map(tile_residual, (coherency, visibility, tile_map))
    return (gains, residual)
```

```python
import functools

import jax
import jax.numpy as jnp
import numpy as np
from jax import lax
from jax.experimental import pallas as pl
from jax.experimental.pallas import tpu as pltpu
from jax.sharding import PartitionSpec as P

S = 512
K = 8
F = 16
P_SIZE = 3
ITERS = 3
SB = 16
BLOCKS = S // SB
QUADS = 4
F32 = jnp.float32
BF16 = jnp.bfloat16


def poly_table(count, terms):
    points = ((2.0 * np.arange(count) + 1.0) / count - 1.0).astype(np.float64)
    columns = []
    for power in range(terms):
        vector = points**power
        for column in columns:
            vector = vector - np.sum(column * vector) * column
        columns.append(vector / np.sqrt(np.sum(vector * vector)))
    return np.stack(columns, 1)


def fit_blocks():
    table = poly_table(F, P_SIZE)
    whole = (table @ table.T).astype(np.float32)
    out = np.zeros((4, 64, 256), np.float32)
    for me in range(4):
        for d in range(4):
            piece = whole[4 * me : 4 * me + 4, 4 * (me ^ d) : 4 * (me ^ d) + 4]
            out[me, :, 64 * d : 64 * d + 64] = np.kron(np.eye(16, dtype=np.float32), piece)
    return out


def mat_mul(a, b):
    re, im = [], []
    for r in range(2):
        for c in range(2):
            x, y, u, v = a[2 * r], a[4 + 2 * r], b[c], b[4 + c]
            x1, y1, u1, v1 = a[2 * r + 1], a[5 + 2 * r], b[2 + c], b[6 + c]
            re.append((x * u - y * v) + (x1 * u1 - y1 * v1))
            im.append((x * v + y * u) + (x1 * v1 + y1 * u1))
    return re + im


def mat_mul_herm(a, b):
    re, im = [], []
    for r in range(2):
        for c in range(2):
            x, y, u, v = a[2 * r], a[4 + 2 * r], b[2 * c], b[4 + 2 * c]
            x1, y1, u1, v1 = a[2 * r + 1], a[5 + 2 * r], b[2 * c + 1], b[5 + 2 * c]
            re.append((x * u + y * v) + (x1 * u1 + y1 * v1))
            im.append((y * u - x * v) + (y1 * u1 - x1 * v1))
    return re + im


def herm_mat_mul(a, b):
    re, im = [], []
    for r in range(2):
        for c in range(2):
            x, y, u, v = a[r], a[4 + r], b[c], b[4 + c]
            x1, y1, u1, v1 = a[2 + r], a[6 + r], b[2 + c], b[6 + c]
            re.append((x * u + y * v) + (x1 * u1 + y1 * v1))
            im.append((x * v - y * u) + (x1 * v1 - y1 * u1))
    return re + im


def square_right(z):
    d0 = (z[0] * z[0] + z[4] * z[4]) + (z[1] * z[1] + z[5] * z[5])
    d1 = (z[2] * z[2] + z[6] * z[6]) + (z[3] * z[3] + z[7] * z[7])
    re = (z[0] * z[2] + z[4] * z[6]) + (z[1] * z[3] + z[5] * z[7])
    im = (z[4] * z[2] - z[0] * z[6]) + (z[5] * z[3] - z[1] * z[7])
    return [d0, d1, re, im]


def square_left(w):
    d0 = (w[0] * w[0] + w[4] * w[4]) + (w[2] * w[2] + w[6] * w[6])
    d1 = (w[1] * w[1] + w[5] * w[5]) + (w[3] * w[3] + w[7] * w[7])
    re = (w[0] * w[1] + w[4] * w[5]) + (w[2] * w[3] + w[6] * w[7])
    im = (w[0] * w[5] - w[4] * w[1]) + (w[2] * w[7] - w[6] * w[3])
    return [d0, d1, re, im]


def three_terms(x):
    hi = x.astype(BF16)
    rest = x - hi.astype(F32)
    mid = rest.astype(BF16)
    return hi, mid, (rest - mid.astype(F32)).astype(BF16)


def dot(a, b, dims):
    return lax.dot_general(a, b, (dims, ((), ())), preferred_element_type=F32)


def pick_matrix(side, copies):
    row = lax.broadcasted_iota(jnp.int32, (16, 256), 0)
    slot = lax.broadcasted_iota(jnp.int32, (16, 256), 1)
    index = slot // 16 if side == 0 else slot % 16
    pick = (row == index).astype(F32)
    return jnp.concatenate([pick] * copies, 0).astype(BF16)


def start_kernel(gains_ref, out_ref, rows_ref):
    rows_ref[...] = jnp.zeros(rows_ref.shape, F32)
    rows_ref[:, 0:8] = gains_ref[...]
    halves = []
    for half in range(2):
        tiles = []
        for quad in (2 * half, 2 * half + 1):
            for c in range(8):
                tiles.append(rows_ref[pl.ds(quad * 64 + c, 8, stride=8), :])
        halves.append(jnp.transpose(jnp.concatenate(tiles, 0))[0:8])
    row = jnp.concatenate(halves, 0)
    for j in range(out_ref.shape[0]):
        out_ref[j] = row


def expand_gains(got_ref, pair_ref):
    parts = three_terms(got_ref[...])
    for side in range(2):
        pick = pick_matrix(side, 3)
        for quad in range(QUADS):
            piece = jnp.concatenate(
                [p[16 * quad : 16 * quad + 16, 128 * side : 128 * side + 64] for p in parts], 0
            )
            pair_ref[side, quad] = dot(piece, pick, ((0,), (0,)))


def station_rows(gall_ref, map_ref, got_ref):
    got_ref[...] = jnp.zeros(got_ref.shape, F32)
    for side in range(2):
        start = pl.multiple_of(map_ref[0, side] * 32, 32)
        rows = gall_ref[pl.ds(start, 32), :]
        for quad in range(QUADS):
            for half in range(2):
                at = 16 * quad + 8 * half
                first = 16 * half + 8 * (quad // 2)
                got_ref[at : at + 8, 128 * side : 128 * side + 64] = rows[
                    first : first + 8, 64 * (quad % 2) : 64 * (quad % 2) + 64
                ]


def load_visibility(vis_ref, v_ref):
    vis = vis_ref[...].astype(F32)
    for h in range(2):
        v_ref[h, 0:64] = vis[:, 128 * h : 128 * h + 128]
        v_ref[h, 64:128] = vis[:, 128 * h : 128 * h + 128]


def over_quads(x):
    return x + pltpu.roll(x, 4, 0)


def tile_terms(coh_ref, vis_ref, flag_ref, map_ref, got_ref, msg_ref, c_ref, v_ref, pair_ref, z_ref, s_ref):
    weight = flag_ref[...].astype(F32)
    for h in range(2):
        at = slice(128 * h, 128 * h + 128)
        c_ref[h] = coh_ref[:, at].astype(F32) * weight[:, at]
    load_visibility(vis_ref, v_ref)
    expand_gains(got_ref, pair_ref)

    def half_step(h, carry):
        lanes = pl.ds(pl.multiple_of(h * 128, 128), 128)
        for t in range(2):
            total = None
            for quad in range(QUADS):
                cs = [c_ref[h, pl.ds(quad * 128 + t * 8 + c, 8, stride=16), :] for c in range(8)]
                gp = [pair_ref[0, quad, 8 * c : 8 * c + 8, lanes] for c in range(8)]
                gq = [pair_ref[1, quad, 8 * c : 8 * c + 8, lanes] for c in range(8)]
                z = mat_mul_herm(cs, gq)
                for c in range(8):
                    z_ref[quad, c] = z[c]
                m = mat_mul(gp, z)
                total = m if total is None else [x + y for x, y in zip(total, m)]
            resid = [
                v_ref[h, pl.ds(t * 8 + c, 8, stride=16), :] - over_quads(total[c])
                for c in range(8)
            ]
            for quad in range(QUADS):
                z = [z_ref[quad, c] for c in range(8)]
                terms_p = mat_mul_herm(resid, z) + square_right(z)
                cs = [c_ref[h, pl.ds(quad * 128 + t * 8 + c, 8, stride=16), :] for c in range(8)]
                gp = [pair_ref[0, quad, 8 * c : 8 * c + 8, lanes] for c in range(8)]
                w = mat_mul(gp, cs)
                terms_q = herm_mat_mul(resid, w) + square_left(w)
                for side, terms in ((0, terms_p), (1, terms_q)):
                    for c in range(12):
                        rows = slice(8 * c, 8 * c + 8)
                        if t == 0:
                            s_ref[side, quad, rows, lanes] = terms[c]
                        else:
                            s_ref[side, quad, rows, lanes] += terms[c]
        return carry

    lax.fori_loop(0, 2, half_step, 0)
    for side in range(2):
        pick = pick_matrix(side, 1)
        spare = jnp.full((16, 32), map_ref[0, side].astype(F32), F32)
        for quad in range(QUADS):
            rows = slice(16 * quad, 16 * quad + 16)
            hi, mid, lo = three_terms(s_ref[side, quad])
            dims = ((1,), (1,))
            msg_ref[rows, 128 * side : 128 * side + 96] = (
                dot(pick, lo, dims) + dot(pick, mid, dims)
            ) + dot(pick, hi, dims)
            msg_ref[rows, 128 * side + 96 : 128 * side + 128] = spare


def first_tile_kernel(
    coh_ref, vis_ref, flag_ref, map_ref, me_ref, gall_ref, msg_ref, own_ref,
    c_ref, v_ref, pair_ref, z_ref, s_ref, got_ref, turn_ref,
):
    quad, row = me_ref[0], me_ref[1]
    first = (row // 8) * 16 + (quad // 2) * 8 + row % 8
    turn_ref[...] = jnp.transpose(gall_ref[pl.ds(first, BLOCKS, stride=32), :])
    own_ref[...] = turn_ref[pl.ds(pl.multiple_of((quad % 2) * 64, 64), 64), :]
    station_rows(gall_ref, map_ref, got_ref)
    tile_terms(coh_ref, vis_ref, flag_ref, map_ref, got_ref, msg_ref, c_ref, v_ref, pair_ref, z_ref, s_ref)


def tile_kernel(
    coh_ref, vis_ref, flag_ref, map_ref, got_ref, msg_ref, c_ref, v_ref, pair_ref, z_ref, s_ref
):
    tile_terms(coh_ref, vis_ref, flag_ref, map_ref, got_ref, msg_ref, c_ref, v_ref, pair_ref, z_ref, s_ref)


def update_kernel(last, got_ref, gains_ref, g1_ref, g2_ref, g3_ref, fit_ref, pen_ref, me_ref, *outs):
    msg_ref = outs[0]
    got = got_ref[...]
    block = lax.broadcasted_iota(jnp.int32, (64, BLOCKS), 1)
    picks = [
        (got[:, 128 * side + 96 : 128 * side + 97].astype(jnp.int32) == block).astype(F32)
        for side in range(2)
    ]
    pick = jnp.concatenate(picks, 0).astype(BF16)
    rows = jnp.concatenate([got[:, 0:128], got[:, 128:256]], 0)
    hi, mid, lo = three_terms(jnp.transpose(rows))
    dims = ((1,), (0,))
    normal = (dot(lo, pick, dims) + dot(mid, pick, dims)) + dot(hi, pick, dims)

    gains = gains_ref[...]
    others = jnp.concatenate([gains, g1_ref[...], g2_ref[...], g3_ref[...]], 0)
    consensus = jnp.dot(
        fit_ref[...], others, precision=lax.Precision.HIGHEST, preferred_element_type=F32
    )
    row = lax.broadcasted_iota(jnp.int32, (8, BLOCKS), 0)
    quad = me_ref[0]
    penalty = jnp.where(row < 4, pen_ref[2 * quad], pen_ref[2 * quad + 1])
    g = [gains[8 * c : 8 * c + 8] for c in range(8)]
    u = [
        normal[8 * c : 8 * c + 8] + penalty * (consensus[8 * c : 8 * c + 8] - g[c])
        for c in range(8)
    ]
    h0 = normal[64:72] + penalty
    h1 = normal[72:80] + penalty
    off_re, off_im = normal[80:88], normal[88:96]
    scale = 1.0 / (h0 * h1 - off_re * off_re - off_im * off_im)
    new_re, new_im = [], []
    for r in range(2):
        x, y, x1, y1 = u[2 * r], u[4 + 2 * r], u[2 * r + 1], u[5 + 2 * r]
        new_re.append(g[2 * r] + (x * h1 - (x1 * off_re + y1 * off_im)) * scale)
        new_re.append(g[2 * r + 1] + (x1 * h0 - (x * off_re - y * off_im)) * scale)
        new_im.append(g[4 + 2 * r] + (y * h1 - (y1 * off_re - x1 * off_im)) * scale)
        new_im.append(g[5 + 2 * r] + (y1 * h0 - (y * off_re + x * off_im)) * scale)
    new = jnp.concatenate(new_re + new_im, 0)
    zeros = jnp.zeros_like(new)
    dims = ((1,), (1,))
    parts = jnp.concatenate(three_terms(jnp.concatenate([new, zeros], 0)), 1)
    sent = dot(jnp.concatenate([pick] * 3, 1), parts, dims)
    if last:
        device = lax.broadcasted_iota(jnp.int32, (64, BLOCKS), 0) // 2
        held = (device == block).astype(F32).astype(BF16)
        parts = jnp.concatenate(three_terms(jnp.concatenate([zeros, new], 0)), 1)
        msg_ref[:, 0:128] = sent[0:64] + dot(jnp.concatenate([held] * 3, 1), parts, dims)
    else:
        outs[1][...] = new
        msg_ref[:, 0:128] = sent[0:64]
    msg_ref[:, 128:256] = sent[64:128]


def last_kernel(
    coh_ref, vis_ref, me_ref, got_ref, gains_ref, resid_ref, c_ref, v_ref, pair_ref, turn_ref, r_ref
):
    half = me_ref[2]
    for quad in range(QUADS):
        rows = got_ref[pl.ds(pl.multiple_of(quad * 16 + half * 8, 8), 8), 0:128]
        turn_ref[:, 0:8] = jnp.transpose(rows)
        for k2 in range(2):
            for f in range(4):
                gains_ref[2 * quad + k2, f] = turn_ref[pl.ds(64 + 4 * k2 + f, 8, stride=8), :][:, 0:8]
    for h in range(2):
        c_ref[h] = coh_ref[:, 128 * h : 128 * h + 128].astype(F32)
    load_visibility(vis_ref, v_ref)
    expand_gains(got_ref, pair_ref)

    def half_step(h, carry):
        lanes = pl.ds(pl.multiple_of(h * 128, 128), 128)
        for t in range(2):
            total = None
            for quad in range(QUADS):
                cs = [c_ref[h, pl.ds(quad * 128 + t * 8 + c, 8, stride=16), :] for c in range(8)]
                gp = [pair_ref[0, quad, 8 * c : 8 * c + 8, lanes] for c in range(8)]
                gq = [pair_ref[1, quad, 8 * c : 8 * c + 8, lanes] for c in range(8)]
                m = mat_mul(gp, mat_mul_herm(cs, gq))
                total = m if total is None else [x + y for x, y in zip(total, m)]
            for c in range(8):
                observed = v_ref[h, pl.ds(t * 8 + c, 8, stride=16), :]
                r_ref[h, pl.ds(t * 8 + c, 8, stride=16), :] = observed - over_quads(total[c])
        return carry

    lax.fori_loop(0, 2, half_step, 0)
    for h in range(2):
        resid_ref[:, 128 * h : 128 * h + 128] = r_ref[h, 0:64].astype(BF16)


VMEM = pl.BlockSpec(memory_space=pltpu.VMEM)
SMEM = pl.BlockSpec(memory_space=pltpu.SMEM)


def call(kernel, in_specs, out_shapes, scratch, flops):
    return pl.pallas_call(
        kernel,
        in_specs=in_specs,
        out_specs=[VMEM] * len(out_shapes),
        out_shape=[jax.ShapeDtypeStruct(s, d) for s, d in out_shapes],
        scratch_shapes=[pltpu.VMEM(s, d) for s, d in scratch],
        compiler_params=pltpu.CompilerParams(vmem_limit_bytes=24 * 1024 * 1024),
        cost_estimate=pl.CostEstimate(flops=flops, bytes_accessed=1 << 19, transcendentals=0),
    )


WORK = [((2, 512, 128), F32), ((2, 128, 128), F32), ((2, QUADS, 64, 256), F32)]
TERMS = [((QUADS, 8, 8, 128), F32), ((2, QUADS, 96, 256), F32)]


def exchange(x):
    return lax.all_to_all(x, "pairs", 0, 0, tiled=True)


def local(coherency, visibility, tile_map, flag_mask, gains_start, penalty):
    pair = lax.axis_index("pairs")
    chan = lax.axis_index("chan")
    me = jnp.stack([pair // 16, pair % 16, pair % 2, chan]).astype(jnp.int32)
    fit = lax.dynamic_index_in_dim(jnp.asarray(fit_blocks()), chan, 0, keepdims=False)
    coh = coherency.reshape(512, 256)
    vis = visibility.reshape(64, 256)

    (spread,) = call(start_kernel, [VMEM], [((64, 16, 128), F32)], [((256, 128), F32)], 1 << 17)(
        gains_start.reshape(256, 8)
    )
    gall = exchange(spread).reshape(2 * S, 128)
    msg, gains = call(
        first_tile_kernel,
        [VMEM, VMEM, VMEM, SMEM, SMEM, VMEM],
        [((64, 256), F32), ((64, BLOCKS), F32)],
        WORK + TERMS + [((64, 256), F32), ((128, BLOCKS), F32)],
        8 << 20,
    )(coh, vis, flag_mask, tile_map, me, gall)
    for sweep in range(ITERS):
        others = [
            lax.ppermute(gains, "chan", [(i, i ^ d) for i in range(4)]) for d in (1, 2, 3)
        ]
        got = exchange(msg)
        last = sweep + 1 == ITERS
        out_shapes = [((64, 256), F32)] + ([] if last else [((64, BLOCKS), F32)])
        out = call(
            functools.partial(update_kernel, last),
            [VMEM] * 6 + [SMEM, SMEM],
            out_shapes,
            [],
            4 << 20,
        )(got, gains, *others, fit, penalty, me)
        back = exchange(out[0])
        if not last:
            gains = out[1]
            (msg,) = call(
                tile_kernel,
                [VMEM, VMEM, VMEM, SMEM, VMEM],
                [((64, 256), F32)],
                WORK + TERMS,
                8 << 20,
            )(coh, vis, flag_mask, tile_map, back)
    solved, residual = call(
        last_kernel,
        [VMEM, VMEM, SMEM, VMEM],
        [((K, 4, 8, 8), F32), ((64, 256), BF16)],
        WORK + [((128, 128), F32), ((2, 128, 128), F32)],
        4 << 20,
    )(coh, vis, me, back)
    return (solved, residual.reshape(visibility.shape))


def solution(mesh):
    in_specs = (
        P("pairs", None, "chan", None, None, None),
        P("pairs", "chan", None, None, None),
        P("pairs", None),
        P("pairs", None),
        P(None, "chan", None, "pairs"),
        P(),
    )
    out_specs = (P(None, "chan", None, "pairs"), P("pairs", "chan", None, None, None))
    return jax.shard_map(local, mesh=mesh, in_specs=in_specs, out_specs=out_specs, check_vma=False)
```

```python
import functools

import jax
import jax.numpy as jnp
import numpy as np
from jax import lax
from jax.experimental import pallas as pl
from jax.experimental.pallas import tpu as pltpu
from jax.sharding import PartitionSpec as P

S = 512
K = 8
F = 16
P_SIZE = 3
ITERS = 3
SB = 16
BLOCKS = S // SB
QUADS = 4
F32 = jnp.float32
BF16 = jnp.bfloat16


def poly_table(count, terms):
    points = ((2.0 * np.arange(count) + 1.0) / count - 1.0).astype(np.float64)
    columns = []
    for power in range(terms):
        vector = points**power
        for column in columns:
            vector = vector - np.sum(column * vector) * column
        columns.append(vector / np.sqrt(np.sum(vector * vector)))
    return np.stack(columns, 1)


def fit_tables():
    table = poly_table(F, P_SIZE)
    whole = table @ table.T
    out = np.zeros((4, 384, 256), np.float64)
    for me in range(4):
        mine = table[4 * me : 4 * me + 4]
        for d in range(4):
            other = me ^ d
            piece = whole[4 * me : 4 * me + 4, 4 * other : 4 * other + 4]
            out[me, 0:64, 64 * d : 64 * d + 64] = np.kron(np.eye(16), piece)
            for c in range(8):
                for k2 in range(2):
                    row = 8 * c + 4 * k2
                    for term in range(P_SIZE):
                        column = 24 * (c // 4) + 8 * term + 2 * (c % 4) + k2
                        out[me, 64 + 64 * d + row : 68 + 64 * d + row, column] = table[
                            4 * other : 4 * other + 4, term
                        ]
                        out[me, 320 + row : 324 + row, column] = mine[:, term]
    return out.astype(np.float32)


def mat_mul(a, b):
    re, im = [], []
    for r in range(2):
        for c in range(2):
            x, y, u, v = a[2 * r], a[4 + 2 * r], b[c], b[4 + c]
            x1, y1, u1, v1 = a[2 * r + 1], a[5 + 2 * r], b[2 + c], b[6 + c]
            re.append((x * u - y * v) + (x1 * u1 - y1 * v1))
            im.append((x * v + y * u) + (x1 * v1 + y1 * u1))
    return re + im


def mat_mul_herm(a, b):
    re, im = [], []
    for r in range(2):
        for c in range(2):
            x, y, u, v = a[2 * r], a[4 + 2 * r], b[2 * c], b[4 + 2 * c]
            x1, y1, u1, v1 = a[2 * r + 1], a[5 + 2 * r], b[2 * c + 1], b[5 + 2 * c]
            re.append((x * u + y * v) + (x1 * u1 + y1 * v1))
            im.append((y * u - x * v) + (y1 * u1 - x1 * v1))
    return re + im


def herm_mat_mul(a, b):
    re, im = [], []
    for r in range(2):
        for c in range(2):
            x, y, u, v = a[r], a[4 + r], b[c], b[4 + c]
            x1, y1, u1, v1 = a[2 + r], a[6 + r], b[2 + c], b[6 + c]
            re.append((x * u + y * v) + (x1 * u1 + y1 * v1))
            im.append((x * v - y * u) + (x1 * v1 - y1 * u1))
    return re + im


def square_right(z):
    d0 = (z[0] * z[0] + z[4] * z[4]) + (z[1] * z[1] + z[5] * z[5])
    d1 = (z[2] * z[2] + z[6] * z[6]) + (z[3] * z[3] + z[7] * z[7])
    re = (z[0] * z[2] + z[4] * z[6]) + (z[1] * z[3] + z[5] * z[7])
    im = (z[4] * z[2] - z[0] * z[6]) + (z[5] * z[3] - z[1] * z[7])
    return [d0, d1, re, im]


def square_left(w):
    d0 = (w[0] * w[0] + w[4] * w[4]) + (w[2] * w[2] + w[6] * w[6])
    d1 = (w[1] * w[1] + w[5] * w[5]) + (w[3] * w[3] + w[7] * w[7])
    re = (w[0] * w[1] + w[4] * w[5]) + (w[2] * w[3] + w[6] * w[7])
    im = (w[0] * w[5] - w[4] * w[1]) + (w[2] * w[7] - w[6] * w[3])
    return [d0, d1, re, im]


def three_terms(x):
    hi = x.astype(BF16)
    rest = x - hi.astype(F32)
    mid = rest.astype(BF16)
    return hi, mid, (rest - mid.astype(F32)).astype(BF16)


def exact_dot(a, b):
    return jnp.dot(a, b, precision=lax.Precision.HIGHEST, preferred_element_type=F32)


def dot(a, b, dims):
    return lax.dot_general(a, b, (dims, ((), ())), preferred_element_type=F32)


def pick_matrix(side, copies):
    row = lax.broadcasted_iota(jnp.int32, (16, 256), 0)
    slot = lax.broadcasted_iota(jnp.int32, (16, 256), 1)
    index = slot // 16 if side == 0 else slot % 16
    pick = (row == index).astype(F32)
    return jnp.concatenate([pick] * copies, 0).astype(BF16)


def start_kernel(gains_ref, out_ref, row_ref, rows_ref):
    rows_ref[...] = jnp.zeros(rows_ref.shape, F32)
    rows_ref[:, 0:8] = gains_ref[...]
    halves = []
    for half in range(2):
        tiles = []
        for quad in (2 * half, 2 * half + 1):
            for c in range(8):
                tiles.append(rows_ref[pl.ds(quad * 64 + c, 8, stride=8), :])
        halves.append(jnp.transpose(jnp.concatenate(tiles, 0))[0:8])
    row = jnp.concatenate(halves, 0)
    row_ref[...] = row
    for j in range(out_ref.shape[0]):
        out_ref[j] = row


def coefficient_kernel(row_ref, r1_ref, r2_ref, r3_ref, tables_ref, out_ref):
    rows = [r[...] for r in (row_ref, r1_ref, r2_ref, r3_ref)]
    halves = [
        jnp.concatenate([r[:, 64 * odd : 64 * odd + 64] for r in rows], 1) for odd in range(2)
    ]
    out_ref[...] = exact_dot(jnp.concatenate(halves, 0), tables_ref[64:320, 0:128])


def expand_gains(got_ref, me_ref, pair_ref, stride):
    for side in range(2):
        pick = pick_matrix(side, 3)
        for quad in range(QUADS):
            rows = got_ref[quad_rows(me_ref, quad, 16, stride), :]
            if side:
                rows = pltpu.roll(rows, 64, 1)
            piece = jnp.concatenate([p[:, 0:64] for p in three_terms(rows)], 0)
            pair_ref[side, quad] = dot(piece, pick, ((0,), (0,)))


def quad_rows(me_ref, quad, count, stride, offset=0):
    start = pl.multiple_of((quad ^ me_ref[5]) * (16 * stride), 16 * stride)
    if stride == 1:
        return pl.ds(start + offset, count)
    return pl.ds(start + offset, count, stride=stride)


def station_rows(gall_ref, me_ref, got_ref):
    for side in range(2):
        start = pl.multiple_of(me_ref[3 + side] * 32, 32)
        rows = gall_ref[pl.ds(start, 32), :]
        for quad in range(QUADS):
            for half in range(2):
                first = 16 * half + 8 * (quad // 2)
                part = rows[first : first + 8]
                if quad % 2 != side:
                    part = pltpu.roll(part, 64, 1)
                at = pl.multiple_of((quad ^ me_ref[5]) * 16 + 8 * half, 8)
                got_ref[pl.ds(at, 8), 64 * side : 64 * side + 64] = part[:, 64 * side : 64 * side + 64]


def load_visibility(vis_ref, v_ref):
    vis = vis_ref[...].astype(F32)
    for h in range(2):
        v_ref[h, 0:64] = vis[:, 128 * h : 128 * h + 128]
        v_ref[h, 64:128] = vis[:, 128 * h : 128 * h + 128]


def over_quads(x):
    return x + pltpu.roll(x, 4, 0)


def tile_terms(
    coh_ref, vis_ref, weight_ref, me_ref, got_ref, coef, msg_ref, c_ref, v_ref, pair_ref, z_ref, s_ref
):
    weight = weight_ref[...]
    for h in range(2):
        at = slice(128 * h, 128 * h + 128)
        c_ref[h] = coh_ref[:, at].astype(F32) * weight[:, at]
    load_visibility(vis_ref, v_ref)
    expand_gains(got_ref, me_ref, pair_ref, 1)

    def half_step(h, carry):
        lanes = pl.ds(pl.multiple_of(h * 128, 128), 128)
        for t in range(2):
            total = None
            for quad in range(QUADS):
                cs = [c_ref[h, pl.ds(quad * 128 + t * 8 + c, 8, stride=16), :] for c in range(8)]
                gp = [pair_ref[0, quad, 8 * c : 8 * c + 8, lanes] for c in range(8)]
                gq = [pair_ref[1, quad, 8 * c : 8 * c + 8, lanes] for c in range(8)]
                z = mat_mul_herm(cs, gq)
                for c in range(8):
                    z_ref[quad, c] = z[c]
                m = mat_mul(gp, z)
                total = m if total is None else [x + y for x, y in zip(total, m)]
            resid = [
                v_ref[h, pl.ds(t * 8 + c, 8, stride=16), :] - over_quads(total[c])
                for c in range(8)
            ]
            for quad in range(QUADS):
                z = [z_ref[quad, c] for c in range(8)]
                terms_p = mat_mul_herm(resid, z) + square_right(z)
                cs = [c_ref[h, pl.ds(quad * 128 + t * 8 + c, 8, stride=16), :] for c in range(8)]
                gp = [pair_ref[0, quad, 8 * c : 8 * c + 8, lanes] for c in range(8)]
                w = mat_mul(gp, cs)
                terms_q = herm_mat_mul(resid, w) + square_left(w)
                for side, terms in ((0, terms_p), (1, terms_q)):
                    for c in range(12):
                        rows = slice(8 * c, 8 * c + 8)
                        if t == 0:
                            s_ref[side, quad, rows, lanes] = terms[c]
                        else:
                            s_ref[side, quad, rows, lanes] += terms[c]
        return carry

    lax.fori_loop(0, 2, half_step, 0)
    for side in range(2):
        pick = pick_matrix(side, 1)
        spare = jnp.full((16, 32 if coef is None else 8), me_ref[3 + side].astype(F32), F32)
        for quad in range(QUADS):
            hi, mid, lo = three_terms(s_ref[side, quad])
            dims = ((1,), (1,))
            sums = (dot(pick, lo, dims) + dot(pick, mid, dims)) + dot(pick, hi, dims)
            parts = [sums, spare]
            if coef is not None:
                first = 16 * (quad % 2) + 8 * (quad // 2)
                mine = coef[first : first + 8, 24 * side : 24 * side + 24]
                parts.append(jnp.concatenate([mine, mine], 0))
            rows = quad_rows(me_ref, quad, 16, 2, side)
            msg_ref[rows, :] = jnp.concatenate(parts, 1)


def first_tile_kernel(
    coh_ref, vis_ref, weight_ref, me_ref, gall_ref, coef_ref, msg_ref, own_ref,
    c_ref, v_ref, pair_ref, z_ref, s_ref, got_ref, turn_ref,
):
    quad, row = me_ref[0], me_ref[1]
    first = (row // 8) * 16 + (quad // 2) * 8 + row % 8
    turn_ref[...] = jnp.transpose(gall_ref[pl.ds(first, BLOCKS, stride=32), :])
    own_ref[...] = turn_ref[pl.ds(pl.multiple_of((quad % 2) * 64, 64), 64), :]
    station_rows(gall_ref, me_ref, got_ref)
    tile_terms(
        coh_ref, vis_ref, weight_ref, me_ref, got_ref, coef_ref[...],
        msg_ref, c_ref, v_ref, pair_ref, z_ref, s_ref,
    )


def tile_kernel(
    coh_ref, vis_ref, weight_ref, me_ref, got_ref, msg_ref, c_ref, v_ref, pair_ref, z_ref, s_ref
):
    tile_terms(
        coh_ref, vis_ref, weight_ref, me_ref, got_ref, None,
        msg_ref, c_ref, v_ref, pair_ref, z_ref, s_ref,
    )


def update_kernel(sweep, got_ref, gains_ref, tables_ref, pen_ref, me_ref, *refs):
    last = sweep + 1 == ITERS
    others, outs = (refs[:3], refs[3:]) if sweep else ((), refs)
    msg_ref = outs[0]
    sides = [got_ref[pl.ds(side, 64, stride=2), :] for side in range(2)]
    block = lax.broadcasted_iota(jnp.int32, (64, BLOCKS), 1)
    picks = [
        (side[:, 96:97].astype(jnp.int32) == block).astype(F32)
        for side in sides
    ]
    pick = jnp.concatenate(picks, 0).astype(BF16)
    turned = jnp.transpose(jnp.concatenate(sides, 0))
    hi, mid, lo = three_terms(turned[0:96])
    dims = ((1,), (0,))
    normal = (dot(lo, pick, dims) + dot(mid, pick, dims)) + dot(hi, pick, dims)

    gains = gains_ref[...]
    device = lax.broadcasted_iota(jnp.int32, (64, BLOCKS), 0)
    if sweep:
        everyone = jnp.concatenate([gains] + [r[...] for r in others], 0)
        consensus = exact_dot(tables_ref[0:64], everyone)
    else:
        held = (device // 2 == block) & (device % 2 == me_ref[1] // 8)
        held = held.astype(F32).astype(BF16)
        hi, mid, lo = three_terms(jnp.concatenate([turned[104:128, 0:64], turned[104:128, 64:128]], 0))
        coef = (dot(lo, held, dims) + dot(mid, held, dims)) + dot(hi, held, dims)
        consensus = exact_dot(tables_ref[320:384, 0:48], coef)
    row = lax.broadcasted_iota(jnp.int32, (8, BLOCKS), 0)
    quad = me_ref[0]
    penalty = jnp.where(row < 4, pen_ref[2 * quad], pen_ref[2 * quad + 1])
    g = [gains[8 * c : 8 * c + 8] for c in range(8)]
    u = [
        normal[8 * c : 8 * c + 8] + penalty * (consensus[8 * c : 8 * c + 8] - g[c])
        for c in range(8)
    ]
    h0 = normal[64:72] + penalty
    h1 = normal[72:80] + penalty
    off_re, off_im = normal[80:88], normal[88:96]
    scale = 1.0 / (h0 * h1 - off_re * off_re - off_im * off_im)
    new_re, new_im = [], []
    for r in range(2):
        x, y, x1, y1 = u[2 * r], u[4 + 2 * r], u[2 * r + 1], u[5 + 2 * r]
        new_re.append(g[2 * r] + (x * h1 - (x1 * off_re + y1 * off_im)) * scale)
        new_re.append(g[2 * r + 1] + (x1 * h0 - (x * off_re - y * off_im)) * scale)
        new_im.append(g[4 + 2 * r] + (y * h1 - (y1 * off_re - x1 * off_im)) * scale)
        new_im.append(g[5 + 2 * r] + (y1 * h0 - (y * off_re + x * off_im)) * scale)
    new = jnp.concatenate(new_re + new_im, 0)
    zeros = jnp.zeros_like(new)
    dims = ((1,), (1,))
    parts = jnp.concatenate(three_terms(jnp.concatenate([new, zeros], 0)), 1)
    other = jnp.concatenate(three_terms(jnp.concatenate([zeros, new], 0)), 1)
    picks = [jnp.concatenate([p.astype(BF16)] * 3, 1) for p in picks]
    sent = dot(picks[0], parts, dims) + dot(picks[1], other, dims)
    if last:
        held = (device // 2 == block).astype(F32).astype(BF16)
        msg_ref[pl.ds(0, 64, stride=2), :] = sent
        msg_ref[pl.ds(1, 64, stride=2), :] = dot(jnp.concatenate([held] * 3, 1), parts, dims)
    else:
        outs[1][...] = new
        msg_ref[...] = sent


def last_kernel(
    coh_ref, vis_ref, me_ref, got_ref, gains_ref, resid_ref, c_ref, v_ref, pair_ref, turn_ref, r_ref
):
    half = me_ref[2]
    for quad in range(QUADS):
        rows = got_ref[quad_rows(me_ref, quad, 8, 2, half * 16 + 1), :]
        turn_ref[:, 0:8] = jnp.transpose(rows)
        for k2 in range(2):
            for f in range(4):
                gains_ref[2 * quad + k2, f] = turn_ref[pl.ds(4 * k2 + f, 8, stride=8), :][:, 0:8]
    for h in range(2):
        c_ref[h] = coh_ref[:, 128 * h : 128 * h + 128].astype(F32)
    load_visibility(vis_ref, v_ref)
    expand_gains(got_ref, me_ref, pair_ref, 2)

    def half_step(h, carry):
        lanes = pl.ds(pl.multiple_of(h * 128, 128), 128)
        for t in range(2):
            total = None
            for quad in range(QUADS):
                cs = [c_ref[h, pl.ds(quad * 128 + t * 8 + c, 8, stride=16), :] for c in range(8)]
                gp = [pair_ref[0, quad, 8 * c : 8 * c + 8, lanes] for c in range(8)]
                gq = [pair_ref[1, quad, 8 * c : 8 * c + 8, lanes] for c in range(8)]
                m = mat_mul(gp, mat_mul_herm(cs, gq))
                total = m if total is None else [x + y for x, y in zip(total, m)]
            for c in range(8):
                observed = v_ref[h, pl.ds(t * 8 + c, 8, stride=16), :]
                r_ref[h, pl.ds(t * 8 + c, 8, stride=16), :] = observed - over_quads(total[c])
        return carry

    lax.fori_loop(0, 2, half_step, 0)
    for h in range(2):
        resid_ref[:, 128 * h : 128 * h + 128] = r_ref[h, 0:64].astype(BF16)


VMEM = pl.BlockSpec(memory_space=pltpu.VMEM)
SMEM = pl.BlockSpec(memory_space=pltpu.SMEM)


def call(kernel, in_specs, out_shapes, scratch, flops):
    return pl.pallas_call(
        kernel,
        in_specs=in_specs,
        out_specs=[VMEM] * len(out_shapes),
        out_shape=[jax.ShapeDtypeStruct(s, d) for s, d in out_shapes],
        scratch_shapes=[pltpu.VMEM(s, d) for s, d in scratch],
        compiler_params=pltpu.CompilerParams(vmem_limit_bytes=24 * 1024 * 1024),
        cost_estimate=pl.CostEstimate(flops=flops, bytes_accessed=1 << 19, transcendentals=0),
    )


WORK = [((2, 512, 128), F32), ((2, 128, 128), F32), ((2, QUADS, 64, 256), F32)]
TERMS = [((QUADS, 8, 8, 128), F32), ((2, QUADS, 96, 256), F32)]


def exchange(x):
    return lax.all_to_all(x, "pairs", 0, 0, tiled=True)


def local(coherency, visibility, tile_map, flag_mask, gains_start, penalty):
    pair = lax.axis_index("pairs")
    chan = lax.axis_index("chan")
    flip = 2 * (chan // 2)
    me = jnp.stack(
        [(pair // 16) ^ flip, pair % 16, pair % 2, tile_map[0, 0], tile_map[0, 1], flip]
    )
    tables = lax.dynamic_index_in_dim(jnp.asarray(fit_tables()), chan, 0, keepdims=False)
    coh = coherency.reshape(512, 256)
    vis = visibility.reshape(64, 256)

    def from_chans(x, flip):
        mask = lambda d: d ^ (128 if flip and d > 1 else 0)
        return [
            lax.ppermute(x, ("pairs", "chan"), [(i, i ^ mask(d)) for i in range(256)])
            for d in (1, 2, 3)
        ]

    spread, row = call(
        start_kernel, [VMEM], [((64, 16, 128), F32), ((16, 128), F32)], [((256, 128), F32)], 1 << 17
    )(gains_start.reshape(256, 8))
    gall = exchange(spread).reshape(2 * S, 128)
    (coef,) = call(coefficient_kernel, [VMEM] * 5, [((32, 128), F32)], [], 1 << 20)(
        row, *from_chans(row, False), tables
    )
    weight = flag_mask.astype(F32)
    gall, coef, tables, weight, me = lax.optimization_barrier((gall, coef, tables, weight, me))
    msg, gains = call(
        first_tile_kernel,
        [VMEM, VMEM, VMEM, SMEM, VMEM, VMEM],
        [((128, 128), F32), ((64, BLOCKS), F32)],
        WORK + TERMS + [((64, 128), F32), ((128, BLOCKS), F32)],
        8 << 20,
    )(coh, vis, weight, me, gall, coef)
    others = []
    for sweep in range(ITERS):
        got = exchange(msg.reshape(64, 2, 128)).reshape(128, 128)
        last = sweep + 1 == ITERS
        out = call(
            functools.partial(update_kernel, sweep),
            [VMEM, VMEM, VMEM, SMEM, SMEM] + [VMEM] * len(others),
            [((128, 128), F32)] if last else [((64, 128), F32), ((64, BLOCKS), F32)],
            [],
            4 << 20,
        )(got, gains, tables, penalty, me, *others)
        back = exchange(out[0].reshape(64, -1, 128)).reshape(-1, 128)
        if not last:
            gains = out[1]
            others = from_chans(gains, True)
            (msg,) = call(
                tile_kernel,
                [VMEM, VMEM, VMEM, SMEM, VMEM],
                [((128, 128), F32)],
                WORK + TERMS,
                8 << 20,
            )(coh, vis, weight, me, back)
            msg, *others = lax.optimization_barrier((msg, *others))
    solved, residual = call(
        last_kernel,
        [VMEM, VMEM, SMEM, VMEM],
        [((K, 4, 8, 8), F32), ((64, 256), BF16)],
        WORK + [((128, 128), F32), ((2, 128, 128), F32)],
        4 << 20,
    )(coh, vis, me, back)
    return (solved, residual.reshape(visibility.shape))


def solution(mesh):
    in_specs = (
        P("pairs", None, "chan", None, None, None),
        P("pairs", "chan", None, None, None),
        P("pairs", None),
        P("pairs", None),
        P(None, "chan", None, "pairs"),
        P(),
    )
    out_specs = (P(None, "chan", None, "pairs"), P("pairs", "chan", None, None, None))
    return jax.shard_map(local, mesh=mesh, in_specs=in_specs, out_specs=out_specs, check_vma=False)
```

```python
import functools

import jax
import jax.numpy as jnp
import numpy as np
from jax import lax
from jax.experimental import pallas as pl
from jax.experimental.pallas import tpu as pltpu
from jax.sharding import PartitionSpec as P

S = 512
K = 8
F = 16
P_SIZE = 3
ITERS = 3
SB = 16
BLOCKS = S // SB
QUADS = 4
STATIONS = 40
F32 = jnp.float32
BF16 = jnp.bfloat16


def poly_table(count, terms):
    points = ((2.0 * np.arange(count) + 1.0) / count - 1.0).astype(np.float64)
    columns = []
    for power in range(terms):
        vector = points**power
        for column in columns:
            vector = vector - np.sum(column * vector) * column
        columns.append(vector / np.sqrt(np.sum(vector * vector)))
    return np.stack(columns, 1)


def fit_tables():
    table = poly_table(F, P_SIZE)
    out = np.zeros((4, 128, 48), np.float32)
    for me in range(4):
        for c in range(8):
            for k2 in range(2):
                row = 8 * c + 4 * k2
                for term in range(P_SIZE):
                    column = 16 * term + 2 * c + k2
                    out[me, row : row + 4, column] = table[4 * me : 4 * me + 4, term]
                    out[me, 64 + row : 68 + row, column] = table[4 * me : 4 * me + 4, term]
    return out


def mat_mul(a, b):
    re, im = [], []
    for r in range(2):
        for c in range(2):
            x, y, u, v = a[2 * r], a[4 + 2 * r], b[c], b[4 + c]
            x1, y1, u1, v1 = a[2 * r + 1], a[5 + 2 * r], b[2 + c], b[6 + c]
            re.append((x * u - y * v) + (x1 * u1 - y1 * v1))
            im.append((x * v + y * u) + (x1 * v1 + y1 * u1))
    return re + im


def mat_mul_herm(a, b):
    re, im = [], []
    for r in range(2):
        for c in range(2):
            x, y, u, v = a[2 * r], a[4 + 2 * r], b[2 * c], b[4 + 2 * c]
            x1, y1, u1, v1 = a[2 * r + 1], a[5 + 2 * r], b[2 * c + 1], b[5 + 2 * c]
            re.append((x * u + y * v) + (x1 * u1 + y1 * v1))
            im.append((y * u - x * v) + (y1 * u1 - x1 * v1))
    return re + im


def herm_mat_mul(a, b):
    re, im = [], []
    for r in range(2):
        for c in range(2):
            x, y, u, v = a[r], a[4 + r], b[c], b[4 + c]
            x1, y1, u1, v1 = a[2 + r], a[6 + r], b[2 + c], b[6 + c]
            re.append((x * u + y * v) + (x1 * u1 + y1 * v1))
            im.append((x * v - y * u) + (x1 * v1 - y1 * u1))
    return re + im


def square_right(z):
    d0 = (z[0] * z[0] + z[4] * z[4]) + (z[1] * z[1] + z[5] * z[5])
    d1 = (z[2] * z[2] + z[6] * z[6]) + (z[3] * z[3] + z[7] * z[7])
    re = (z[0] * z[2] + z[4] * z[6]) + (z[1] * z[3] + z[5] * z[7])
    im = (z[4] * z[2] - z[0] * z[6]) + (z[5] * z[3] - z[1] * z[7])
    return [d0, d1, re, im]


def square_left(w):
    d0 = (w[0] * w[0] + w[4] * w[4]) + (w[2] * w[2] + w[6] * w[6])
    d1 = (w[1] * w[1] + w[5] * w[5]) + (w[3] * w[3] + w[7] * w[7])
    re = (w[0] * w[1] + w[4] * w[5]) + (w[2] * w[3] + w[6] * w[7])
    im = (w[0] * w[5] - w[4] * w[1]) + (w[2] * w[7] - w[6] * w[3])
    return [d0, d1, re, im]


def three_terms(x):
    hi = x.astype(BF16)
    rest = x - hi.astype(F32)
    mid = rest.astype(BF16)
    return hi, mid, (rest - mid.astype(F32)).astype(BF16)


def dot(a, b, dims):
    return lax.dot_general(a, b, (dims, ((), ())), preferred_element_type=F32)


def exact_dot(a, b, dims):
    return lax.dot_general(
        a, b, (dims, ((), ())), precision=lax.Precision.HIGHEST, preferred_element_type=F32
    )


def slot_index(side, rows):
    slot = lax.broadcasted_iota(jnp.int32, (rows, 256), 1)
    return slot // 16 if side == 0 else slot % 16


def start_kernel(gains_hbm, map_hbm, out_ref, gains_ref, map_ref, rows_ref, sem):
    copies = [
        pltpu.make_async_copy(gains_hbm, gains_ref, sem.at[0]),
        pltpu.make_async_copy(map_hbm, map_ref, sem.at[1]),
    ]
    for copy in copies:
        copy.start()
    rows_ref[...] = jnp.zeros(rows_ref.shape, F32)
    for copy in copies:
        copy.wait()
    rows_ref[:, 0:8] = gains_ref[...]
    parts = []
    for half in range(2):
        tiles = []
        for quad in (2 * half, 2 * half + 1):
            for c in range(8):
                tiles.append(rows_ref[pl.ds(quad * 64 + c, 8, stride=8), :])
        parts.append(jnp.transpose(jnp.concatenate(tiles, 0))[0:8])
    lane = lax.broadcasted_iota(jnp.int32, (1, 128), 1)
    blocks = map_ref[...].astype(F32)
    parts.append(jnp.where(lane == 0, blocks[:, 0:1], blocks[:, 1:2]))
    eight = jnp.concatenate(parts * 8, 0)
    for group in range(8):
        out_ref[136 * group : 136 * group + 136] = eight


def spread_kernel(coh_ref, vis_ref, weight_ref, plain_ref, masked_ref, observed_ref, c_ref, v_ref):
    vis = vis_ref[...].astype(F32)
    for h in range(2):
        at = slice(128 * h, 128 * h + 128)
        c_ref[h] = coh_ref[:, at].astype(F32)
        v_ref[h, 0:64] = vis[:, at]
        v_ref[h, 64:128] = vis[:, at]
        weight = weight_ref[:, at]
        for t in range(2):
            for c in range(8):
                observed_ref[h, t, c] = v_ref[h, pl.ds(t * 8 + c, 8, stride=16), :]
                for quad in range(QUADS):
                    rows = c_ref[h, pl.ds(quad * 128 + t * 8 + c, 8, stride=16), :]
                    plain_ref[h, t, quad, c] = rows
                    masked_ref[h, t, quad, c] = rows * weight


def over_quads(x):
    return x + pltpu.roll(x, 4, 0)


def expand_gains(gains, pair_ref):
    station = lax.broadcasted_iota(jnp.int32, (STATIONS, 256), 0)
    picks = [
        (station - 16 * side == slot_index(side, STATIONS)).astype(F32) for side in range(2)
    ]
    picks[0] = jnp.where(station < 16, picks[0], 0.0)
    picks[1] = jnp.where((station >= 16) & (station < 32), picks[1], 0.0)
    pick = jnp.concatenate([jnp.concatenate(picks, 1)] * 3, 0).astype(BF16)
    pair_ref[...] = dot(jnp.concatenate(three_terms(gains), 1), pick, ((1,), (0,)))


def coefficients(gains, tables_ref, coef_ref):
    coef_ref[...] = jnp.concatenate(
        [
            exact_dot(gains[64 * quad : 64 * quad + 64], tables_ref[0:64], ((0,), (0,)))
            for quad in range(QUADS)
        ],
        1,
    )


def tile_terms(c_ref, v_ref, msg_ref, pair_ref, z_ref, s_ref):
    def half_step(h, carry):
        lanes = pl.ds(pl.multiple_of(h * 128, 128), 128)
        lanes_q = pl.ds(pl.multiple_of(h * 128 + 256, 128), 128)
        for t in range(2):
            total = None
            for quad in range(QUADS):
                cs = [c_ref[h, t, quad, c] for c in range(8)]
                rows = [slice(64 * quad + 8 * c, 64 * quad + 8 * c + 8) for c in range(8)]
                gp = [pair_ref[r, lanes] for r in rows]
                gq = [pair_ref[r, lanes_q] for r in rows]
                z = mat_mul_herm(cs, gq)
                for c in range(8):
                    z_ref[quad, c] = z[c]
                m = mat_mul(gp, z)
                total = m if total is None else [x + y for x, y in zip(total, m)]
            resid = [
                v_ref[h, t, c] - over_quads(total[c])
                for c in range(8)
            ]
            for quad in range(QUADS):
                z = [z_ref[quad, c] for c in range(8)]
                terms_p = mat_mul_herm(resid, z) + square_right(z)
                cs = [c_ref[h, t, quad, c] for c in range(8)]
                gp = [pair_ref[64 * quad + 8 * c : 64 * quad + 8 * c + 8, lanes] for c in range(8)]
                w = mat_mul(gp, cs)
                terms_q = herm_mat_mul(resid, w) + square_left(w)
                for side, terms in ((0, terms_p), (1, terms_q)):
                    for c in range(12):
                        rows = slice(96 * quad + 8 * c, 96 * quad + 8 * c + 8)
                        if t == 0:
                            s_ref[side, rows, lanes] = terms[c]
                        else:
                            s_ref[side, rows, lanes] += terms[c]
        return carry

    lax.fori_loop(0, 2, half_step, 0)
    row = lax.broadcasted_iota(jnp.int32, (16, 256), 0)
    for side in range(2):
        pick = (row == slot_index(side, 16)).astype(F32).astype(BF16)
        for chunk in range(3):
            hi, mid, lo = three_terms(s_ref[side, 128 * chunk : 128 * chunk + 128])
            dims = ((1,), (1,))
            sums = (dot(pick, lo, dims) + dot(pick, mid, dims)) + dot(pick, hi, dims)
            at = 48 * side + 16 * chunk
            for copy in range(8):
                msg_ref[copy, at : at + 16] = sums


def first_tile_kernel(
    c_ref, v_ref, gall_ref, tables_ref, msg_ref, gains_ref, coef_ref,
    pair_ref, z_ref, s_ref,
):
    pair = lax.axis_index("pairs")
    tile = gall_ref[pl.ds(17 * pair + 16, 1), :].astype(jnp.int32)
    a, b = 34 * tile[0, 0], 34 * tile[0, 1]
    starts = [a, a + 17, b, b + 17, 17 * pair]
    turned = []
    for half in range(2):
        rows = [gall_ref[pl.ds(start + 8 * half, 8), :] for start in starts]
        turned.append(jnp.transpose(jnp.concatenate(rows, 0)))
    gains = jnp.concatenate(turned, 0)
    gains_ref[...] = gains
    expand_gains(gains, pair_ref)
    tile_terms(c_ref, v_ref, msg_ref, pair_ref, z_ref, s_ref)
    coefficients(gains_ref[...], tables_ref, coef_ref)


def share_kernel(got_ref, plan_ref, out_ref, table_ref):
    level = lax.axis_index("pairs") % 8
    half = pl.multiple_of(8 * (level % 2), 8)
    blocks = [[plan_ref[n, side] for side in range(2)] for n in range(16)]
    table_ref[...] = jnp.zeros(table_ref.shape, F32)
    for z in range(8):
        for side in range(2):
            table_ref[blocks[z][side]] += got_ref[z, 48 * side : 48 * side + 48]
    for target in range(8):
        out_ref[target, 0:48] = table_ref[blocks[8 + target][0]]
        out_ref[target, 48:96] = table_ref[blocks[8 + target][1]]
        for chunk in range(3):
            at = 96 + 8 * chunk
            rows = pl.ds(16 * chunk + half, 8)
            out_ref[target, at : at + 8] = table_ref[4 * target + level // 2, rows, :]


def update_gains(got_ref, gains_ref, coefs, tables_ref, pen_ref):
    sums = got_ref[0]
    for n in range(1, 8):
        sums = sums + got_ref[n]
    turned = []
    for chunk in range(3):
        at = 16 * chunk
        rows = [sums[at : at + 16], sums[48 + at : 64 + at], sums[96 + 8 * chunk : 104 + 8 * chunk]]
        turned.append(jnp.transpose(jnp.concatenate(rows, 0)))
    normal = jnp.concatenate(turned, 0)
    coef = coefs[0][...] + coefs[1][...]
    new = []
    for quad in range(QUADS):
        consensus = exact_dot(
            tables_ref[64:128], coef[:, 48 * quad : 48 * quad + 48], ((1,), (1,))
        )
        penalty = pen_ref[8 * quad : 8 * quad + 8, 0:STATIONS]
        g = [gains_ref[64 * quad + 8 * c : 64 * quad + 8 * c + 8] for c in range(8)]
        n = [normal[96 * quad + 8 * c : 96 * quad + 8 * c + 8] for c in range(12)]
        u = [n[c] + penalty * (consensus[8 * c : 8 * c + 8] - g[c]) for c in range(8)]
        h0, h1, off_re, off_im = n[8] + penalty, n[9] + penalty, n[10], n[11]
        scale = 1.0 / (h0 * h1 - off_re * off_re - off_im * off_im)
        new_re, new_im = [], []
        for r in range(2):
            x, y, x1, y1 = u[2 * r], u[4 + 2 * r], u[2 * r + 1], u[5 + 2 * r]
            new_re.append(g[2 * r] + (x * h1 - (x1 * off_re + y1 * off_im)) * scale)
            new_re.append(g[2 * r + 1] + (x1 * h0 - (x * off_re - y * off_im)) * scale)
            new_im.append(g[4 + 2 * r] + (y * h1 - (y1 * off_re - x1 * off_im)) * scale)
            new_im.append(g[5 + 2 * r] + (y1 * h0 - (y * off_re + x * off_im)) * scale)
        new += new_re + new_im
    return jnp.concatenate(new, 0)


def tile_kernel(
    c_ref, v_ref, pen_ref, got_ref, gains_ref, near_ref, far_ref, tables_ref,
    msg_ref, new_ref, coef_ref, pair_ref, z_ref, s_ref,
):
    gains = update_gains(got_ref, gains_ref, (near_ref, far_ref), tables_ref, pen_ref)
    new_ref[...] = gains
    expand_gains(gains, pair_ref)
    tile_terms(c_ref, v_ref, msg_ref, pair_ref, z_ref, s_ref)
    coefficients(new_ref[...], tables_ref, coef_ref)


def last_kernel(
    c_ref, v_ref, pen_ref, got_ref, gains_ref, near_ref, far_ref, tables_ref,
    solved_ref, resid_ref, pair_ref, turn_ref, r_ref,
):
    gains = update_gains(got_ref, gains_ref, (near_ref, far_ref), tables_ref, pen_ref)
    turn_ref[:, 0:STATIONS] = gains
    for quad in range(QUADS):
        for k2 in range(2):
            for f in range(4):
                rows = turn_ref[pl.ds(64 * quad + 4 * k2 + f, 8, stride=8), :]
                solved_ref[2 * quad + k2, f] = rows[:, 32:40]
    expand_gains(gains, pair_ref)

    def half_step(h, carry):
        lanes = pl.ds(pl.multiple_of(h * 128, 128), 128)
        lanes_q = pl.ds(pl.multiple_of(h * 128 + 256, 128), 128)
        for t in range(2):
            total = None
            for quad in range(QUADS):
                cs = [c_ref[h, t, quad, c] for c in range(8)]
                rows = [slice(64 * quad + 8 * c, 64 * quad + 8 * c + 8) for c in range(8)]
                m = mat_mul(
                    [pair_ref[r, lanes] for r in rows],
                    mat_mul_herm(cs, [pair_ref[r, lanes_q] for r in rows]),
                )
                total = m if total is None else [x + y for x, y in zip(total, m)]
            for c in range(8):
                observed = v_ref[h, t, c]
                r_ref[h, pl.ds(t * 8 + c, 8, stride=16), :] = observed - over_quads(total[c])
        return carry

    lax.fori_loop(0, 2, half_step, 0)
    for h in range(2):
        resid_ref[:, 128 * h : 128 * h + 128] = r_ref[h, 0:64].astype(BF16)


VMEM = pl.BlockSpec(memory_space=pltpu.VMEM)
SMEM = pl.BlockSpec(memory_space=pltpu.SMEM)


def call(kernel, in_specs, out_shapes, scratch, flops, limit=24):
    return pl.pallas_call(
        kernel,
        in_specs=in_specs,
        out_specs=[VMEM] * len(out_shapes),
        out_shape=[jax.ShapeDtypeStruct(s, d) for s, d in out_shapes],
        scratch_shapes=[pltpu.VMEM(*s) if isinstance(s, tuple) else s for s in scratch],
        compiler_params=pltpu.CompilerParams(vmem_limit_bytes=limit * 1024 * 1024),
        cost_estimate=pl.CostEstimate(flops=flops, bytes_accessed=1 << 19, transcendentals=0),
    )


WORK = [((256, 512), F32)]
TERMS = [((QUADS, 8, 8, 128), F32), ((2, 384, 256), F32)]
TILE_OUT = [((8, 96, 128), F32), ((256, STATIONS), F32), ((STATIONS, 192), F32)]
ALONG_Z = [[8 * column + z for z in range(8)] for column in range(8)]
ACROSS = [[8 * column + z for column in range(8)] for z in range(8)]


def exchange(x, groups=None):
    return lax.all_to_all(x, "pairs", 0, 0, tiled=True, axis_index_groups=groups)


def local(coherency, visibility, tile_map, flag_mask, gains_start, penalty):
    pair = lax.axis_index("pairs")
    chan = lax.axis_index("chan")
    tables = lax.dynamic_index_in_dim(jnp.asarray(fit_tables()), chan, 0, keepdims=False)
    coh = coherency.reshape(512, 256)
    vis = visibility.reshape(64, 256)
    weight = flag_mask.astype(F32)

    def from_chan(x, d):
        return lax.ppermute(x, "chan", [(i, i ^ d) for i in range(4)])

    (spread,) = call(
        start_kernel,
        [pl.BlockSpec(memory_space=pl.ANY)] * 2,
        [((64 * 17, 128), F32)],
        [((256, 8), F32), ((1, 2), jnp.int32), ((256, 128), F32), pltpu.SemaphoreType.DMA((2,))],
        1 << 17,
        60,
    )(gains_start.reshape(256, 8), tile_map)
    gall = exchange(spread.reshape(64, 17, 1, 128)).reshape(64 * 17, 128)
    penalty = jnp.broadcast_to(jnp.repeat(penalty, 4)[:, None], (32, 128))
    plain, masked, observed = call(
        spread_kernel,
        [VMEM] * 3,
        [((2, 2, QUADS, 8, 8, 128), F32)] * 2 + [((2, 2, 8, 8, 128), F32)],
        [((2, 512, 128), F32), ((2, 128, 128), F32)],
        1 << 20,
    )(coh, vis, weight)
    gall, tables, penalty, plain, masked, observed = lax.optimization_barrier(
        (gall, tables, penalty, plain, masked, observed)
    )
    maps = gall.reshape(8, 8, 17, 128)[:, :, 16, 0:2].astype(jnp.int32)
    plan = jnp.concatenate(
        [
            lax.dynamic_index_in_dim(maps, pair // 8, 0, keepdims=False),
            lax.dynamic_index_in_dim(maps, pair % 8, 1, keepdims=False),
        ],
        0,
    )
    msg, gains, coef = call(
        first_tile_kernel,
        [VMEM] * 4,
        TILE_OUT,
        WORK + TERMS,
        8 << 20,
    )(masked, observed, gall, tables)
    for sweep in range(ITERS):
        got = exchange(msg, ALONG_Z)
        near = coef + from_chan(coef, 1)
        coefs = [near, from_chan(near, 2)]
        got, plan, *coefs = lax.optimization_barrier((got, plan, *coefs))
        (share,) = call(
            share_kernel, [VMEM, VMEM], [((8, 120, 128), F32)], [((BLOCKS, 48, 128), F32)], 1 << 20
        )(got, plan)
        sums = exchange(share, ACROSS)
        if sweep + 1 < ITERS:
            msg, gains, coef = call(
                tile_kernel,
                [VMEM] * 8,
                TILE_OUT,
                WORK + TERMS,
                8 << 20,
            )(masked, observed, penalty, sums, gains, *coefs, tables)
    solved, residual = call(
        last_kernel,
        [VMEM] * 8,
        [((K, 4, 8, 8), F32), ((64, 256), BF16)],
        WORK + [((256, 128), F32), ((2, 128, 128), F32)],
        4 << 20,
    )(plain, observed, penalty, sums, gains, *coefs, tables)
    return (solved, residual.reshape(visibility.shape))


def solution(mesh):
    in_specs = (
        P("pairs", None, "chan", None, None, None),
        P("pairs", "chan", None, None, None),
        P("pairs", None),
        P("pairs", None),
        P(None, "chan", None, "pairs"),
        P(),
    )
    out_specs = (P(None, "chan", None, "pairs"), P("pairs", "chan", None, None, None))
    return jax.shard_map(local, mesh=mesh, in_specs=in_specs, out_specs=out_specs, check_vma=False)
```

```python
import functools

import jax
import jax.numpy as jnp
import numpy as np
from jax import lax
from jax.experimental import pallas as pl
from jax.experimental.pallas import tpu as pltpu
from jax.sharding import PartitionSpec as P

S = 512
K = 8
F = 16
P_SIZE = 3
ITERS = 3
SB = 16
BLOCKS = S // SB
QUADS = 4
STATIONS = 40
F32 = jnp.float32
BF16 = jnp.bfloat16


def poly_table(count, terms):
    points = ((2.0 * np.arange(count) + 1.0) / count - 1.0).astype(np.float64)
    columns = []
    for power in range(terms):
        vector = points**power
        for column in columns:
            vector = vector - np.sum(column * vector) * column
        columns.append(vector / np.sqrt(np.sum(vector * vector)))
    return np.stack(columns, 1)


def fit_tables():
    table = poly_table(F, P_SIZE)
    out = np.zeros((4, 128, 48), np.float32)
    for me in range(4):
        for c in range(8):
            for k2 in range(2):
                row = 8 * c + 4 * k2
                for term in range(P_SIZE):
                    column = 16 * term + 2 * c + k2
                    out[me, row : row + 4, column] = table[4 * me : 4 * me + 4, term]
                    out[me, 64 + row : 68 + row, column] = table[4 * me : 4 * me + 4, term]
    return out


def mat_mul(a, b):
    re, im = [], []
    for r in range(2):
        for c in range(2):
            x, y, u, v = a[2 * r], a[4 + 2 * r], b[c], b[4 + c]
            x1, y1, u1, v1 = a[2 * r + 1], a[5 + 2 * r], b[2 + c], b[6 + c]
            re.append((x * u - y * v) + (x1 * u1 - y1 * v1))
            im.append((x * v + y * u) + (x1 * v1 + y1 * u1))
    return re + im


def mat_mul_herm(a, b):
    re, im = [], []
    for r in range(2):
        for c in range(2):
            x, y, u, v = a[2 * r], a[4 + 2 * r], b[2 * c], b[4 + 2 * c]
            x1, y1, u1, v1 = a[2 * r + 1], a[5 + 2 * r], b[2 * c + 1], b[5 + 2 * c]
            re.append((x * u + y * v) + (x1 * u1 + y1 * v1))
            im.append((y * u - x * v) + (y1 * u1 - x1 * v1))
    return re + im


def herm_mat_mul(a, b):
    re, im = [], []
    for r in range(2):
        for c in range(2):
            x, y, u, v = a[r], a[4 + r], b[c], b[4 + c]
            x1, y1, u1, v1 = a[2 + r], a[6 + r], b[2 + c], b[6 + c]
            re.append((x * u + y * v) + (x1 * u1 + y1 * v1))
            im.append((x * v - y * u) + (x1 * v1 - y1 * u1))
    return re + im


def square_right(z):
    d0 = (z[0] * z[0] + z[4] * z[4]) + (z[1] * z[1] + z[5] * z[5])
    d1 = (z[2] * z[2] + z[6] * z[6]) + (z[3] * z[3] + z[7] * z[7])
    re = (z[0] * z[2] + z[4] * z[6]) + (z[1] * z[3] + z[5] * z[7])
    im = (z[4] * z[2] - z[0] * z[6]) + (z[5] * z[3] - z[1] * z[7])
    return [d0, d1, re, im]


def square_left(w):
    d0 = (w[0] * w[0] + w[4] * w[4]) + (w[2] * w[2] + w[6] * w[6])
    d1 = (w[1] * w[1] + w[5] * w[5]) + (w[3] * w[3] + w[7] * w[7])
    re = (w[0] * w[1] + w[4] * w[5]) + (w[2] * w[3] + w[6] * w[7])
    im = (w[0] * w[5] - w[4] * w[1]) + (w[2] * w[7] - w[6] * w[3])
    return [d0, d1, re, im]


def three_terms(x):
    hi = x.astype(BF16)
    rest = x - hi.astype(F32)
    mid = rest.astype(BF16)
    return hi, mid, (rest - mid.astype(F32)).astype(BF16)


def dot(a, b, dims):
    return lax.dot_general(a, b, (dims, ((), ())), preferred_element_type=F32)


def exact_dot(a, b, dims):
    return lax.dot_general(
        a, b, (dims, ((), ())), precision=lax.Precision.HIGHEST, preferred_element_type=F32
    )


def slot_index(side, rows):
    slot = lax.broadcasted_iota(jnp.int32, (rows, 256), 1)
    return slot // 16 if side == 0 else slot % 16


def start_kernel(gains_hbm, map_hbm, out_ref, gains_ref, map_ref, rows_ref, sem):
    copies = [
        pltpu.make_async_copy(gains_hbm, gains_ref, sem.at[0]),
        pltpu.make_async_copy(map_hbm, map_ref, sem.at[1]),
    ]
    for copy in copies:
        copy.start()
    rows_ref[...] = jnp.zeros(rows_ref.shape, F32)
    for copy in copies:
        copy.wait()
    rows_ref[:, 0:8] = gains_ref[...]
    parts = []
    for half in range(2):
        tiles = []
        for quad in (2 * half, 2 * half + 1):
            for c in range(8):
                tiles.append(rows_ref[pl.ds(quad * 64 + c, 8, stride=8), :])
        parts.append(jnp.transpose(jnp.concatenate(tiles, 0))[0:8])
    lane = lax.broadcasted_iota(jnp.int32, (1, 128), 1)
    blocks = map_ref[...].astype(F32)
    parts.append(jnp.where(lane == 0, blocks[:, 0:1], blocks[:, 1:2]))
    eight = jnp.concatenate(parts * 8, 0)
    for group in range(8):
        out_ref[136 * group : 136 * group + 136] = eight


def spread_kernel(
    coh_ref, vis_ref, weight_ref, plain_ref, masked_ref, observed_ref, expand_ref, reduce_ref, c_ref, v_ref
):
    pick_tables(expand_ref, reduce_ref)
    vis = vis_ref[...].astype(F32)
    for h in range(2):
        at = slice(128 * h, 128 * h + 128)
        c_ref[h] = coh_ref[:, at].astype(F32)
        v_ref[h, 0:64] = vis[:, at]
        v_ref[h, 64:128] = vis[:, at]
        weight = weight_ref[:, at]
        for t in range(2):
            for c in range(8):
                observed_ref[h, t, c] = v_ref[h, pl.ds(t * 8 + c, 8, stride=16), :]
                for quad in range(QUADS):
                    rows = c_ref[h, pl.ds(quad * 128 + t * 8 + c, 8, stride=16), :]
                    plain_ref[h, t, quad, c] = rows
                    masked_ref[h, t, quad, c] = rows * weight


def over_quads(x):
    return x + pltpu.roll(x, 4, 0)


def pick_tables(expand_ref, reduce_ref):
    station = lax.broadcasted_iota(jnp.int32, (STATIONS, 256), 0)
    picks = []
    for side in range(2):
        pick = (station - 16 * side == slot_index(side, STATIONS)).astype(F32)
        inside = (station >= 16 * side) & (station < 16 * side + 16)
        picks.append(jnp.where(inside, pick, 0.0))
    pick = jnp.concatenate(picks, 1)
    rest = jnp.zeros((128 - 3 * STATIONS, 512), F32)
    expand_ref[...] = jnp.concatenate([pick] * 3 + [rest], 0).astype(BF16)
    row = lax.broadcasted_iota(jnp.int32, (16, 256), 0)
    rows = [(row == slot_index(side, 16)).astype(F32) for side in range(2)]
    reduce_ref[...] = jnp.concatenate(rows, 0).astype(BF16)


def expand_gains(gains, pick_ref, pair_ref):
    rest = jnp.zeros((256, 128 - 3 * STATIONS), F32)
    terms = [term.astype(F32) for term in three_terms(gains)]
    pair_ref[...] = dot(
        jnp.concatenate(terms + [rest], 1).astype(BF16), pick_ref[...], ((1,), (0,))
    )


def coefficients(gains, tables_ref, coef_ref):
    coef_ref[...] = jnp.concatenate(
        [
            exact_dot(gains[64 * quad : 64 * quad + 64], tables_ref[0:64], ((0,), (0,)))
            for quad in range(QUADS)
        ],
        1,
    )


def tile_terms(c_ref, v_ref, pick_ref, msg_ref, pair_ref, z_ref, s_ref):
    def half_step(h, carry):
        lanes = pl.ds(pl.multiple_of(h * 128, 128), 128)
        lanes_q = pl.ds(pl.multiple_of(h * 128 + 256, 128), 128)
        for t in range(2):
            total = None
            for quad in range(QUADS):
                cs = [c_ref[h, t, quad, c] for c in range(8)]
                rows = [slice(64 * quad + 8 * c, 64 * quad + 8 * c + 8) for c in range(8)]
                gp = [pair_ref[r, lanes] for r in rows]
                gq = [pair_ref[r, lanes_q] for r in rows]
                z = mat_mul_herm(cs, gq)
                for c in range(8):
                    z_ref[quad, c] = z[c]
                m = mat_mul(gp, z)
                total = m if total is None else [x + y for x, y in zip(total, m)]
            resid = [
                v_ref[h, t, c] - over_quads(total[c])
                for c in range(8)
            ]
            for quad in range(QUADS):
                z = [z_ref[quad, c] for c in range(8)]
                terms_p = mat_mul_herm(resid, z) + square_right(z)
                cs = [c_ref[h, t, quad, c] for c in range(8)]
                gp = [pair_ref[64 * quad + 8 * c : 64 * quad + 8 * c + 8, lanes] for c in range(8)]
                w = mat_mul(gp, cs)
                terms_q = herm_mat_mul(resid, w) + square_left(w)
                for side, terms in ((0, terms_p), (1, terms_q)):
                    for c in range(12):
                        rows = slice(96 * quad + 8 * c, 96 * quad + 8 * c + 8)
                        if t == 0:
                            s_ref[side, rows, lanes] = terms[c]
                        else:
                            s_ref[side, rows, lanes] += terms[c]
        return carry

    lax.fori_loop(0, 2, half_step, 0)
    def sums(side, first, count):
        terms = s_ref[side, first : first + count]
        hi = terms.astype(BF16)
        lo = (terms - hi.astype(F32)).astype(BF16)
        pick = pick_ref[16 * side : 16 * side + 16]
        return dot(pick, lo, ((1,), (1,))) + dot(pick, hi, ((1,), (1,)))

    for half in range(2):
        first = 192 * half
        rest = [sums(side, first + 128, 64) for side in range(2)]
        parts = [sums(0, first, 128), sums(1, first, 128), jnp.concatenate(rest, 1)]
        for n, part in enumerate(parts):
            for z in range(8):
                msg_ref[8 * half + z, 16 * n : 16 * n + 16] = part


def first_tile_kernel(
    c_ref, v_ref, expand_ref, reduce_ref, gall_ref, tables_ref, msg_ref, gains_ref, coef_ref,
    pair_ref, z_ref, s_ref,
):
    pair = lax.axis_index("pairs")
    tile = gall_ref[pl.ds(17 * pair + 16, 1), :].astype(jnp.int32)
    a, b = 34 * tile[0, 0], 34 * tile[0, 1]
    starts = [a, a + 17, b, b + 17, 17 * pair]
    turned = []
    for half in range(2):
        rows = [gall_ref[pl.ds(start + 8 * half, 8), :] for start in starts]
        turned.append(jnp.transpose(jnp.concatenate(rows, 0)))
    gains = jnp.concatenate(turned, 0)
    gains_ref[...] = gains
    expand_gains(gains, expand_ref, pair_ref)
    tile_terms(c_ref, v_ref, reduce_ref, msg_ref, pair_ref, z_ref, s_ref)
    coefficients(gains_ref[...], tables_ref, coef_ref)


def share_kernel(got_ref, plan_ref, out_ref, table_ref):
    level = lax.axis_index("pairs") % 8
    half = pl.multiple_of(8 * (level % 2), 8)
    blocks = [[plan_ref[n, side] for side in range(2)] for n in range(24)]
    table_ref[...] = jnp.zeros(table_ref.shape, F32)
    for n in range(16):
        rest = got_ref[n, 32:48]
        table_ref[blocks[n][0], 0:16] += got_ref[n, 0:16]
        table_ref[blocks[n][0], 16:32] += rest
        table_ref[blocks[n][1], 0:16] += got_ref[n, 16:32]
        table_ref[blocks[n][1], 16:32] += pltpu.roll(rest, 64, 1)
    lane = lax.broadcasted_iota(jnp.int32, (16, 128), 1)
    for target in range(8):
        a, b = blocks[16 + target]
        own = 4 * target + level // 2
        out_ref[target, 0:16] = table_ref[a, 0:16]
        out_ref[target, 16:32] = table_ref[b, 0:16]
        out_ref[target, 32:48] = jnp.where(
            lane < 64, table_ref[a, 16:32], pltpu.roll(table_ref[b, 16:32], 64, 1)
        )
        out_ref[target, 48:56] = table_ref[own, pl.ds(half, 8), :]
        out_ref[target, 56:64] = table_ref[own, pl.ds(16 + half, 8), :]


def update_gains(got_ref, gains_ref, coefs, tables_ref, pen_ref):
    turned = []
    for half in range(2):
        sums = got_ref[4 * half]
        for n in range(1, 4):
            sums = sums + got_ref[4 * half + n]
        rest = sums[32:48]
        first = jnp.concatenate([sums[0:32], sums[48:56]], 0)
        rest = jnp.concatenate([rest, pltpu.roll(rest, 64, 1), sums[56:64]], 0)
        turned += [jnp.transpose(first), jnp.transpose(rest)[0:64]]
    normal = jnp.concatenate(turned, 0)
    coef = coefs[0][...] + coefs[1][...]
    new = []
    for quad in range(QUADS):
        consensus = exact_dot(
            tables_ref[64:128], coef[:, 48 * quad : 48 * quad + 48], ((1,), (1,))
        )
        penalty = pen_ref[8 * quad : 8 * quad + 8, 0:STATIONS]
        g = [gains_ref[64 * quad + 8 * c : 64 * quad + 8 * c + 8] for c in range(8)]
        n = [normal[96 * quad + 8 * c : 96 * quad + 8 * c + 8] for c in range(12)]
        u = [n[c] + penalty * (consensus[8 * c : 8 * c + 8] - g[c]) for c in range(8)]
        h0, h1, off_re, off_im = n[8] + penalty, n[9] + penalty, n[10], n[11]
        scale = 1.0 / (h0 * h1 - off_re * off_re - off_im * off_im)
        new_re, new_im = [], []
        for r in range(2):
            x, y, x1, y1 = u[2 * r], u[4 + 2 * r], u[2 * r + 1], u[5 + 2 * r]
            new_re.append(g[2 * r] + (x * h1 - (x1 * off_re + y1 * off_im)) * scale)
            new_re.append(g[2 * r + 1] + (x1 * h0 - (x * off_re - y * off_im)) * scale)
            new_im.append(g[4 + 2 * r] + (y * h1 - (y1 * off_re - x1 * off_im)) * scale)
            new_im.append(g[5 + 2 * r] + (y1 * h0 - (y * off_re + x * off_im)) * scale)
        new += new_re + new_im
    return jnp.concatenate(new, 0)


def tile_kernel(
    c_ref, v_ref, expand_ref, reduce_ref, pen_ref, got_ref, gains_ref, near_ref, far_ref, tables_ref,
    msg_ref, new_ref, coef_ref, pair_ref, z_ref, s_ref,
):
    gains = update_gains(got_ref, gains_ref, (near_ref, far_ref), tables_ref, pen_ref)
    new_ref[...] = gains
    expand_gains(gains, expand_ref, pair_ref)
    tile_terms(c_ref, v_ref, reduce_ref, msg_ref, pair_ref, z_ref, s_ref)
    coefficients(new_ref[...], tables_ref, coef_ref)


def last_kernel(
    c_ref, v_ref, expand_ref, pen_ref, got_ref, gains_ref, near_ref, far_ref, tables_ref,
    solved_ref, resid_ref, pair_ref, turn_ref, r_ref,
):
    gains = update_gains(got_ref, gains_ref, (near_ref, far_ref), tables_ref, pen_ref)
    turn_ref[:, 0:STATIONS] = gains
    for quad in range(QUADS):
        for k2 in range(2):
            for f in range(4):
                rows = turn_ref[pl.ds(64 * quad + 4 * k2 + f, 8, stride=8), :]
                solved_ref[2 * quad + k2, f] = rows[:, 32:40]
    expand_gains(gains, expand_ref, pair_ref)

    def half_step(h, carry):
        lanes = pl.ds(pl.multiple_of(h * 128, 128), 128)
        lanes_q = pl.ds(pl.multiple_of(h * 128 + 256, 128), 128)
        for t in range(2):
            total = None
            for quad in range(QUADS):
                cs = [c_ref[h, t, quad, c] for c in range(8)]
                rows = [slice(64 * quad + 8 * c, 64 * quad + 8 * c + 8) for c in range(8)]
                m = mat_mul(
                    [pair_ref[r, lanes] for r in rows],
                    mat_mul_herm(cs, [pair_ref[r, lanes_q] for r in rows]),
                )
                total = m if total is None else [x + y for x, y in zip(total, m)]
            for c in range(8):
                observed = v_ref[h, t, c]
                r_ref[h, pl.ds(t * 8 + c, 8, stride=16), :] = observed - over_quads(total[c])
        return carry

    lax.fori_loop(0, 2, half_step, 0)
    for h in range(2):
        resid_ref[:, 128 * h : 128 * h + 128] = r_ref[h, 0:64].astype(BF16)


VMEM = pl.BlockSpec(memory_space=pltpu.VMEM)
SMEM = pl.BlockSpec(memory_space=pltpu.SMEM)


def call(kernel, in_specs, out_shapes, scratch, flops, limit=24):
    return pl.pallas_call(
        kernel,
        in_specs=in_specs,
        out_specs=[VMEM] * len(out_shapes),
        out_shape=[jax.ShapeDtypeStruct(s, d) for s, d in out_shapes],
        scratch_shapes=[pltpu.VMEM(*s) if isinstance(s, tuple) else s for s in scratch],
        compiler_params=pltpu.CompilerParams(vmem_limit_bytes=limit * 1024 * 1024),
        cost_estimate=pl.CostEstimate(flops=flops, bytes_accessed=1 << 19, transcendentals=0),
    )


WORK = [((256, 512), F32)]
TERMS = [((QUADS, 8, 8, 128), F32), ((2, 384, 256), F32)]
TILE_OUT = [((16, 48, 128), F32), ((256, STATIONS), F32), ((STATIONS, 192), F32)]
ALONG_XZ = [[32 * x + 8 * y + z for x in range(2) for z in range(8)] for y in range(4)]
ACROSS = [[8 * column + z for column in range(8)] for z in range(8)]


def exchange(x, groups=None):
    return lax.all_to_all(x, "pairs", 0, 0, tiled=True, axis_index_groups=groups)


def local(coherency, visibility, tile_map, flag_mask, gains_start, penalty):
    pair = lax.axis_index("pairs")
    chan = lax.axis_index("chan")
    tables = lax.dynamic_index_in_dim(jnp.asarray(fit_tables()), chan, 0, keepdims=False)
    coh = coherency.reshape(512, 256)
    vis = visibility.reshape(64, 256)
    weight = flag_mask.astype(F32)

    def from_chan(x, d):
        return lax.ppermute(x, "chan", [(i, i ^ d) for i in range(4)])

    (spread,) = call(
        start_kernel,
        [pl.BlockSpec(memory_space=pl.ANY)] * 2,
        [((64 * 17, 128), F32)],
        [((256, 8), F32), ((1, 2), jnp.int32), ((256, 128), F32), pltpu.SemaphoreType.DMA((2,))],
        1 << 17,
        60,
    )(gains_start.reshape(256, 8), tile_map)
    gall = exchange(spread.reshape(64, 17, 1, 128)).reshape(64 * 17, 128)
    penalty = jnp.broadcast_to(jnp.repeat(penalty, 4)[:, None], (32, 128))
    plain, masked, observed, expand, reduce = call(
        spread_kernel,
        [VMEM] * 3,
        [((2, 2, QUADS, 8, 8, 128), F32)] * 2
        + [((2, 2, 8, 8, 128), F32), ((128, 512), BF16), ((32, 256), BF16)],
        [((2, 512, 128), F32), ((2, 128, 128), F32)],
        1 << 20,
    )(coh, vis, weight)
    gall, tables, penalty, plain, masked, observed, expand, reduce = lax.optimization_barrier(
        (gall, tables, penalty, plain, masked, observed, expand, reduce)
    )
    maps = gall.reshape(8, 8, 17, 128)[:, :, 16, 0:2].astype(jnp.int32)
    plan = jnp.concatenate(
        [
            lax.dynamic_index_in_dim(
                maps.reshape(2, 4, 8, 2), pair // 8 % 4, 1, keepdims=False
            ).reshape(16, 2),
            lax.dynamic_index_in_dim(maps, pair % 8, 1, keepdims=False),
        ],
        0,
    )
    msg, gains, coef = call(
        first_tile_kernel,
        [VMEM] * 6,
        TILE_OUT,
        WORK + TERMS,
        8 << 20,
    )(masked, observed, expand, reduce, gall, tables)
    for sweep in range(ITERS):
        got = exchange(msg, ALONG_XZ)
        near = coef + from_chan(coef, 1)
        coefs = [near, from_chan(near, 2)]
        got, plan, *coefs = lax.optimization_barrier((got, plan, *coefs))
        (share,) = call(
            share_kernel, [VMEM, VMEM], [((8, 64, 128), F32)], [((BLOCKS, 32, 128), F32)], 1 << 20
        )(got, plan)
        sums = exchange(share, ACROSS)
        if sweep + 1 < ITERS:
            msg, gains, coef = call(
                tile_kernel,
                [VMEM] * 10,
                TILE_OUT,
                WORK + TERMS,
                8 << 20,
            )(masked, observed, expand, reduce, penalty, sums, gains, *coefs, tables)
    solved, residual = call(
        last_kernel,
        [VMEM] * 9,
        [((K, 4, 8, 8), F32), ((64, 256), BF16)],
        WORK + [((256, 128), F32), ((2, 128, 128), F32)],
        4 << 20,
    )(plain, observed, expand, penalty, sums, gains, *coefs, tables)
    return (solved, residual.reshape(visibility.shape))


def solution(mesh):
    in_specs = (
        P("pairs", None, "chan", None, None, None),
        P("pairs", "chan", None, None, None),
        P("pairs", None),
        P("pairs", None),
        P(None, "chan", None, "pairs"),
        P(),
    )
    out_specs = (P(None, "chan", None, "pairs"), P("pairs", "chan", None, None, None))
    return jax.shard_map(local, mesh=mesh, in_specs=in_specs, out_specs=out_specs, check_vma=False)
```

```python
import functools

import jax
import jax.numpy as jnp
import numpy as np
from jax import lax
from jax.experimental import pallas as pl
from jax.experimental.pallas import tpu as pltpu
from jax.sharding import PartitionSpec as P

S = 512
K = 8
F = 16
P_SIZE = 3
ITERS = 3
SB = 16
BLOCKS = S // SB
QUADS = 4
STATIONS = 40
F32 = jnp.float32
BF16 = jnp.bfloat16


def poly_table(count, terms):
    points = ((2.0 * np.arange(count) + 1.0) / count - 1.0).astype(np.float64)
    columns = []
    for power in range(terms):
        vector = points**power
        for column in columns:
            vector = vector - np.sum(column * vector) * column
        columns.append(vector / np.sqrt(np.sum(vector * vector)))
    return np.stack(columns, 1)


def fit_tables():
    table = poly_table(F, P_SIZE)
    out = np.zeros((4, 128, 48), np.float32)
    for me in range(4):
        for c in range(8):
            for k2 in range(2):
                row = 8 * c + 4 * k2
                for term in range(P_SIZE):
                    column = 16 * term + 2 * c + k2
                    out[me, row : row + 4, column] = table[4 * me : 4 * me + 4, term]
                    out[me, 64 + row : 68 + row, column] = table[4 * me : 4 * me + 4, term]
    return out


def mat_mul(a, b):
    re, im = [], []
    for r in range(2):
        for c in range(2):
            x, y, u, v = a[2 * r], a[4 + 2 * r], b[c], b[4 + c]
            x1, y1, u1, v1 = a[2 * r + 1], a[5 + 2 * r], b[2 + c], b[6 + c]
            re.append((x * u - y * v) + (x1 * u1 - y1 * v1))
            im.append((x * v + y * u) + (x1 * v1 + y1 * u1))
    return re + im


def mat_mul_herm(a, b):
    re, im = [], []
    for r in range(2):
        for c in range(2):
            x, y, u, v = a[2 * r], a[4 + 2 * r], b[2 * c], b[4 + 2 * c]
            x1, y1, u1, v1 = a[2 * r + 1], a[5 + 2 * r], b[2 * c + 1], b[5 + 2 * c]
            re.append((x * u + y * v) + (x1 * u1 + y1 * v1))
            im.append((y * u - x * v) + (y1 * u1 - x1 * v1))
    return re + im


def herm_mat_mul(a, b):
    re, im = [], []
    for r in range(2):
        for c in range(2):
            x, y, u, v = a[r], a[4 + r], b[c], b[4 + c]
            x1, y1, u1, v1 = a[2 + r], a[6 + r], b[2 + c], b[6 + c]
            re.append((x * u + y * v) + (x1 * u1 + y1 * v1))
            im.append((x * v - y * u) + (x1 * v1 - y1 * u1))
    return re + im


def square_right(z):
    d0 = (z[0] * z[0] + z[4] * z[4]) + (z[1] * z[1] + z[5] * z[5])
    d1 = (z[2] * z[2] + z[6] * z[6]) + (z[3] * z[3] + z[7] * z[7])
    re = (z[0] * z[2] + z[4] * z[6]) + (z[1] * z[3] + z[5] * z[7])
    im = (z[4] * z[2] - z[0] * z[6]) + (z[5] * z[3] - z[1] * z[7])
    return [d0, d1, re, im]


def square_left(w):
    d0 = (w[0] * w[0] + w[4] * w[4]) + (w[2] * w[2] + w[6] * w[6])
    d1 = (w[1] * w[1] + w[5] * w[5]) + (w[3] * w[3] + w[7] * w[7])
    re = (w[0] * w[1] + w[4] * w[5]) + (w[2] * w[3] + w[6] * w[7])
    im = (w[0] * w[5] - w[4] * w[1]) + (w[2] * w[7] - w[6] * w[3])
    return [d0, d1, re, im]


def three_terms(x):
    hi = x.astype(BF16)
    rest = x - hi.astype(F32)
    mid = rest.astype(BF16)
    return hi, mid, (rest - mid.astype(F32)).astype(BF16)


def dot(a, b, dims):
    return lax.dot_general(a, b, (dims, ((), ())), preferred_element_type=F32)


def exact_dot(a, b, dims):
    return lax.dot_general(
        a, b, (dims, ((), ())), precision=lax.Precision.HIGHEST, preferred_element_type=F32
    )


def copies_kernel(line_ref, out_ref):
    for column in range(8):
        out_ref[column] = line_ref[...]


def slot_index(side, rows):
    slot = lax.broadcasted_iota(jnp.int32, (rows, 256), 1)
    return slot // 16 if side == 0 else slot % 16


def start_kernel(gains_hbm, map_hbm, out_ref, gains_ref, map_ref, rows_ref, sem):
    copies = [pltpu.make_async_copy(map_hbm, map_ref, sem.at[4])]
    for n in range(4):
        rows = pl.ds(64 * n, 64)
        copies.append(pltpu.make_async_copy(gains_hbm.at[rows], gains_ref.at[rows], sem.at[n]))
    for copy in copies:
        copy.start()
    rows_ref[...] = jnp.zeros(rows_ref.shape, F32)
    for copy in copies:
        copy.wait()
    rows_ref[:, 0:8] = gains_ref[...]
    parts = []
    for half in range(2):
        tiles = []
        for quad in (2 * half, 2 * half + 1):
            for c in range(8):
                tiles.append(rows_ref[pl.ds(quad * 64 + c, 8, stride=8), :])
        parts.append(jnp.transpose(jnp.concatenate(tiles, 0))[0:8])
    lane = lax.broadcasted_iota(jnp.int32, (1, 128), 1)
    blocks = map_ref[...].astype(F32)
    parts.append(jnp.where(lane == 0, blocks[:, 0:1], blocks[:, 1:2]))
    out_ref[...] = jnp.concatenate(parts * 8, 0)


def spread_kernel(
    coh_ref, vis_ref, weight_ref, plain_ref, masked_ref, observed_ref, expand_ref, reduce_ref, c_ref, v_ref
):
    pick_tables(expand_ref, reduce_ref)
    vis = vis_ref[...].astype(F32)
    for h in range(2):
        at = slice(128 * h, 128 * h + 128)
        c_ref[h] = coh_ref[:, at].astype(F32)
        v_ref[h, 0:64] = vis[:, at]
        v_ref[h, 64:128] = vis[:, at]
        weight = weight_ref[:, at]
        for t in range(2):
            for c in range(8):
                observed_ref[h, t, c] = v_ref[h, pl.ds(t * 8 + c, 8, stride=16), :]
                for quad in range(QUADS):
                    rows = c_ref[h, pl.ds(quad * 128 + t * 8 + c, 8, stride=16), :]
                    plain_ref[h, t, quad, c] = rows
                    masked_ref[h, t, quad, c] = rows * weight


def over_quads(x):
    return x + pltpu.roll(x, 4, 0)


def pick_tables(expand_ref, reduce_ref):
    station = lax.broadcasted_iota(jnp.int32, (STATIONS, 256), 0)
    picks = []
    for side in range(2):
        pick = (station - 16 * side == slot_index(side, STATIONS)).astype(F32)
        inside = (station >= 16 * side) & (station < 16 * side + 16)
        picks.append(jnp.where(inside, pick, 0.0))
    pick = jnp.concatenate(picks, 1)
    rest = jnp.zeros((128 - 3 * STATIONS, 512), F32)
    expand_ref[...] = jnp.concatenate([pick] * 3 + [rest], 0).astype(BF16)
    row = lax.broadcasted_iota(jnp.int32, (16, 256), 0)
    rows = [(row == slot_index(side, 16)).astype(F32) for side in range(2)]
    reduce_ref[...] = jnp.concatenate(rows, 0).astype(BF16)


def expand_gains(gains, pick_ref, pair_ref):
    rest = jnp.zeros((256, 128 - 3 * STATIONS), F32)
    terms = [term.astype(F32) for term in three_terms(gains)]
    pair_ref[...] = dot(
        jnp.concatenate(terms + [rest], 1).astype(BF16), pick_ref[...], ((1,), (0,))
    )


def coefficients(gains, tables_ref, coef_ref):
    coef_ref[...] = jnp.concatenate(
        [
            exact_dot(gains[64 * quad : 64 * quad + 64], tables_ref[0:64], ((0,), (0,)))
            for quad in range(QUADS)
        ],
        1,
    )


def tile_terms(c_ref, v_ref, pick_ref, msg_ref, pair_ref, z_ref, s_ref):
    def half_step(h, carry):
        lanes = pl.ds(pl.multiple_of(h * 128, 128), 128)
        lanes_q = pl.ds(pl.multiple_of(h * 128 + 256, 128), 128)
        for t in range(2):
            total = None
            for quad in range(QUADS):
                cs = [c_ref[h, t, quad, c] for c in range(8)]
                rows = [slice(64 * quad + 8 * c, 64 * quad + 8 * c + 8) for c in range(8)]
                gp = [pair_ref[r, lanes] for r in rows]
                gq = [pair_ref[r, lanes_q] for r in rows]
                z = mat_mul_herm(cs, gq)
                for c in range(8):
                    z_ref[quad, c] = z[c]
                m = mat_mul(gp, z)
                total = m if total is None else [x + y for x, y in zip(total, m)]
            resid = [
                v_ref[h, t, c] - over_quads(total[c])
                for c in range(8)
            ]
            for quad in range(QUADS):
                z = [z_ref[quad, c] for c in range(8)]
                terms_p = mat_mul_herm(resid, z) + square_right(z)
                cs = [c_ref[h, t, quad, c] for c in range(8)]
                gp = [pair_ref[64 * quad + 8 * c : 64 * quad + 8 * c + 8, lanes] for c in range(8)]
                w = mat_mul(gp, cs)
                terms_q = herm_mat_mul(resid, w) + square_left(w)
                for side, terms in ((0, terms_p), (1, terms_q)):
                    for c in range(12):
                        rows = slice(96 * quad + 8 * c, 96 * quad + 8 * c + 8)
                        if t == 0:
                            s_ref[side, rows, lanes] = terms[c]
                        else:
                            s_ref[side, rows, lanes] += terms[c]
        return carry

    lax.fori_loop(0, 2, half_step, 0)
    def sums(side, first, count):
        terms = s_ref[side, first : first + count]
        hi = terms.astype(BF16)
        lo = (terms - hi.astype(F32)).astype(BF16)
        pick = pick_ref[16 * side : 16 * side + 16]
        return dot(pick, lo, ((1,), (1,))) + dot(pick, hi, ((1,), (1,)))

    for half in range(2):
        first = 192 * half
        rest = [sums(side, first + 128, 64) for side in range(2)]
        parts = [sums(0, first, 128), sums(1, first, 128), jnp.concatenate(rest, 1)]
        for n, part in enumerate(parts):
            for z in range(8):
                msg_ref[8 * half + z, 16 * n : 16 * n + 16] = part


def first_tile_kernel(
    c_ref, v_ref, expand_ref, reduce_ref, gall_ref, tables_ref, msg_ref, gains_ref, coef_ref,
    pair_ref, z_ref, s_ref,
):
    pair = lax.axis_index("pairs")
    tile = gall_ref[pl.ds(17 * pair + 16, 1), :].astype(jnp.int32)
    a, b = 34 * tile[0, 0], 34 * tile[0, 1]
    starts = [a, a + 17, b, b + 17, 17 * pair]
    turned = []
    for half in range(2):
        rows = [gall_ref[pl.ds(start + 8 * half, 8), :] for start in starts]
        turned.append(jnp.transpose(jnp.concatenate(rows, 0)))
    gains = jnp.concatenate(turned, 0)
    gains_ref[...] = gains
    expand_gains(gains, expand_ref, pair_ref)
    tile_terms(c_ref, v_ref, reduce_ref, msg_ref, pair_ref, z_ref, s_ref)
    coefficients(gains_ref[...], tables_ref, coef_ref)


def share_kernel(got_ref, plan_ref, out_ref, table_ref):
    level = lax.axis_index("pairs") % 8
    half = pl.multiple_of(8 * (level % 2), 8)
    blocks = [[plan_ref[n, side] for side in range(2)] for n in range(24)]
    table_ref[...] = jnp.zeros(table_ref.shape, F32)
    for n in range(16):
        rest = got_ref[n, 32:48]
        table_ref[blocks[n][0], 0:16] += got_ref[n, 0:16]
        table_ref[blocks[n][0], 16:32] += rest
        table_ref[blocks[n][1], 0:16] += got_ref[n, 16:32]
        table_ref[blocks[n][1], 16:32] += pltpu.roll(rest, 64, 1)
    lane = lax.broadcasted_iota(jnp.int32, (16, 128), 1)
    for target in range(8):
        a, b = blocks[16 + target]
        own = 4 * target + level // 2
        out_ref[target, 0:16] = table_ref[a, 0:16]
        out_ref[target, 16:32] = table_ref[b, 0:16]
        out_ref[target, 32:48] = jnp.where(
            lane < 64, table_ref[a, 16:32], pltpu.roll(table_ref[b, 16:32], 64, 1)
        )
        out_ref[target, 48:56] = table_ref[own, pl.ds(half, 8), :]
        out_ref[target, 56:64] = table_ref[own, pl.ds(16 + half, 8), :]


def update_gains(got_ref, gains_ref, coefs, tables_ref, pen_ref):
    turned = []
    for half in range(2):
        sums = got_ref[4 * half]
        for n in range(1, 4):
            sums = sums + got_ref[4 * half + n]
        rest = sums[32:48]
        first = jnp.concatenate([sums[0:32], sums[48:56]], 0)
        rest = jnp.concatenate([rest, pltpu.roll(rest, 64, 1), sums[56:64]], 0)
        turned += [jnp.transpose(first), jnp.transpose(rest)[0:64]]
    normal = jnp.concatenate(turned, 0)
    coef = coefs[0][...] + coefs[1][...]
    new = []
    for quad in range(QUADS):
        consensus = exact_dot(
            tables_ref[64:128], coef[:, 48 * quad : 48 * quad + 48], ((1,), (1,))
        )
        penalty = pen_ref[8 * quad : 8 * quad + 8, 0:STATIONS]
        g = [gains_ref[64 * quad + 8 * c : 64 * quad + 8 * c + 8] for c in range(8)]
        n = [normal[96 * quad + 8 * c : 96 * quad + 8 * c + 8] for c in range(12)]
        u = [n[c] + penalty * (consensus[8 * c : 8 * c + 8] - g[c]) for c in range(8)]
        h0, h1, off_re, off_im = n[8] + penalty, n[9] + penalty, n[10], n[11]
        scale = 1.0 / (h0 * h1 - off_re * off_re - off_im * off_im)
        new_re, new_im = [], []
        for r in range(2):
            x, y, x1, y1 = u[2 * r], u[4 + 2 * r], u[2 * r + 1], u[5 + 2 * r]
            new_re.append(g[2 * r] + (x * h1 - (x1 * off_re + y1 * off_im)) * scale)
            new_re.append(g[2 * r + 1] + (x1 * h0 - (x * off_re - y * off_im)) * scale)
            new_im.append(g[4 + 2 * r] + (y * h1 - (y1 * off_re - x1 * off_im)) * scale)
            new_im.append(g[5 + 2 * r] + (y1 * h0 - (y * off_re + x * off_im)) * scale)
        new += new_re + new_im
    return jnp.concatenate(new, 0)


def tile_kernel(
    c_ref, v_ref, expand_ref, reduce_ref, pen_ref, got_ref, gains_ref, near_ref, far_ref, tables_ref,
    msg_ref, new_ref, coef_ref, pair_ref, z_ref, s_ref,
):
    gains = update_gains(got_ref, gains_ref, (near_ref, far_ref), tables_ref, pen_ref)
    new_ref[...] = gains
    expand_gains(gains, expand_ref, pair_ref)
    tile_terms(c_ref, v_ref, reduce_ref, msg_ref, pair_ref, z_ref, s_ref)
    coefficients(new_ref[...], tables_ref, coef_ref)


def last_kernel(
    c_ref, v_ref, expand_ref, pen_ref, got_ref, gains_ref, near_ref, far_ref, tables_ref,
    solved_ref, resid_ref, pair_ref, turn_ref, r_ref,
):
    gains = update_gains(got_ref, gains_ref, (near_ref, far_ref), tables_ref, pen_ref)
    turn_ref[:, 0:STATIONS] = gains
    for quad in range(QUADS):
        for k2 in range(2):
            for f in range(4):
                rows = turn_ref[pl.ds(64 * quad + 4 * k2 + f, 8, stride=8), :]
                solved_ref[2 * quad + k2, f] = rows[:, 32:40]
    expand_gains(gains, expand_ref, pair_ref)

    def half_step(h, carry):
        lanes = pl.ds(pl.multiple_of(h * 128, 128), 128)
        lanes_q = pl.ds(pl.multiple_of(h * 128 + 256, 128), 128)
        for t in range(2):
            total = None
            for quad in range(QUADS):
                cs = [c_ref[h, t, quad, c] for c in range(8)]
                rows = [slice(64 * quad + 8 * c, 64 * quad + 8 * c + 8) for c in range(8)]
                m = mat_mul(
                    [pair_ref[r, lanes] for r in rows],
                    mat_mul_herm(cs, [pair_ref[r, lanes_q] for r in rows]),
                )
                total = m if total is None else [x + y for x, y in zip(total, m)]
            for c in range(8):
                observed = v_ref[h, t, c]
                r_ref[h, pl.ds(t * 8 + c, 8, stride=16), :] = observed - over_quads(total[c])
        return carry

    lax.fori_loop(0, 2, half_step, 0)
    for h in range(2):
        resid_ref[:, 128 * h : 128 * h + 128] = r_ref[h, 0:64].astype(BF16)


VMEM = pl.BlockSpec(memory_space=pltpu.VMEM)
SMEM = pl.BlockSpec(memory_space=pltpu.SMEM)


def call(kernel, in_specs, out_shapes, scratch, flops, limit=24):
    return pl.pallas_call(
        kernel,
        in_specs=in_specs,
        out_specs=[VMEM] * len(out_shapes),
        out_shape=[jax.ShapeDtypeStruct(s, d) for s, d in out_shapes],
        scratch_shapes=[pltpu.VMEM(*s) if isinstance(s, tuple) else s for s in scratch],
        compiler_params=pltpu.CompilerParams(vmem_limit_bytes=limit * 1024 * 1024),
        cost_estimate=pl.CostEstimate(flops=flops, bytes_accessed=1 << 19, transcendentals=0),
    )


WORK = [((256, 512), F32)]
TERMS = [((QUADS, 8, 8, 128), F32), ((2, 384, 256), F32)]
TILE_OUT = [((16, 48, 128), F32), ((256, STATIONS), F32), ((STATIONS, 192), F32)]
ALONG_Z = [[8 * column + z for z in range(8)] for column in range(8)]
ALONG_XZ = [[32 * x + 8 * y + z for x in range(2) for z in range(8)] for y in range(4)]
ACROSS = [[8 * column + z for column in range(8)] for z in range(8)]


def exchange(x, groups=None):
    return lax.all_to_all(x, "pairs", 0, 0, tiled=True, axis_index_groups=groups)


def local(coherency, visibility, tile_map, flag_mask, gains_start, penalty):
    pair = lax.axis_index("pairs")
    chan = lax.axis_index("chan")
    tables = lax.dynamic_index_in_dim(jnp.asarray(fit_tables()), chan, 0, keepdims=False)
    coh = coherency.reshape(512, 256)
    vis = visibility.reshape(64, 256)
    weight = flag_mask.astype(F32)

    def from_chan(x, d):
        return lax.ppermute(x, "chan", [(i, i ^ d) for i in range(4)])

    (spread,) = call(
        start_kernel,
        [pl.BlockSpec(memory_space=pl.ANY)] * 2,
        [((8 * 17, 128), F32)],
        [((256, 8), F32), ((1, 2), jnp.int32), ((256, 128), F32), pltpu.SemaphoreType.DMA((5,))],
        1 << 17,
        60,
    )(gains_start.reshape(256, 8), tile_map)
    line = exchange(spread.reshape(8, 17, 1, 128), ALONG_Z).reshape(136, 128)
    (lines,) = call(copies_kernel, [VMEM], [((8, 136, 128), F32)], [], 1 << 16)(line)
    gall = exchange(lines, ACROSS).reshape(64 * 17, 128)
    penalty = jnp.broadcast_to(jnp.repeat(penalty, 4)[:, None], (32, 128))
    plain, masked, observed, expand, reduce = call(
        spread_kernel,
        [VMEM] * 3,
        [((2, 2, QUADS, 8, 8, 128), F32)] * 2
        + [((2, 2, 8, 8, 128), F32), ((128, 512), BF16), ((32, 256), BF16)],
        [((2, 512, 128), F32), ((2, 128, 128), F32)],
        1 << 20,
    )(coh, vis, weight)
    gall, tables, penalty, plain, masked, observed, expand, reduce = lax.optimization_barrier(
        (gall, tables, penalty, plain, masked, observed, expand, reduce)
    )
    maps = gall.reshape(8, 8, 17, 128)[:, :, 16, 0:2].astype(jnp.int32)
    plan = jnp.concatenate(
        [
            lax.dynamic_index_in_dim(
                maps.reshape(2, 4, 8, 2), pair // 8 % 4, 1, keepdims=False
            ).reshape(16, 2),
            lax.dynamic_index_in_dim(maps, pair % 8, 1, keepdims=False),
        ],
        0,
    )
    msg, gains, coef = call(
        first_tile_kernel,
        [VMEM] * 6,
        TILE_OUT,
        WORK + TERMS,
        8 << 20,
    )(masked, observed, expand, reduce, gall, tables)
    for sweep in range(ITERS):
        got = exchange(msg, ALONG_XZ)
        near = coef + from_chan(coef, 1)
        coefs = [near, from_chan(near, 2)]
        got, plan, *coefs = lax.optimization_barrier((got, plan, *coefs))
        (share,) = call(
            share_kernel, [VMEM, VMEM], [((8, 64, 128), F32)], [((BLOCKS, 32, 128), F32)], 1 << 20
        )(got, plan)
        sums = exchange(share, ACROSS)
        if sweep + 1 < ITERS:
            msg, gains, coef = call(
                tile_kernel,
                [VMEM] * 10,
                TILE_OUT,
                WORK + TERMS,
                8 << 20,
            )(masked, observed, expand, reduce, penalty, sums, gains, *coefs, tables)
    solved, residual = call(
        last_kernel,
        [VMEM] * 9,
        [((K, 4, 8, 8), F32), ((64, 256), BF16)],
        WORK + [((256, 128), F32), ((2, 128, 128), F32)],
        4 << 20,
    )(plain, observed, expand, penalty, sums, gains, *coefs, tables)
    return (solved, residual.reshape(visibility.shape))


def solution(mesh):
    in_specs = (
        P("pairs", None, "chan", None, None, None),
        P("pairs", "chan", None, None, None),
        P("pairs", None),
        P("pairs", None),
        P(None, "chan", None, "pairs"),
        P(),
    )
    out_specs = (P(None, "chan", None, "pairs"), P("pairs", "chan", None, None, None))
    return jax.shard_map(local, mesh=mesh, in_specs=in_specs, out_specs=out_specs, check_vma=False)
```

```python
import functools

import jax
import jax.numpy as jnp
import numpy as np
from jax import lax
from jax.experimental import pallas as pl
from jax.experimental.pallas import tpu as pltpu
from jax.sharding import PartitionSpec as P

S = 512
K = 8
F = 16
P_SIZE = 3
ITERS = 3
SB = 16
BLOCKS = S // SB
QUADS = 4
STATIONS = 40
F32 = jnp.float32
BF16 = jnp.bfloat16


def poly_table(count, terms):
    points = ((2.0 * np.arange(count) + 1.0) / count - 1.0).astype(np.float64)
    columns = []
    for power in range(terms):
        vector = points**power
        for column in columns:
            vector = vector - np.sum(column * vector) * column
        columns.append(vector / np.sqrt(np.sum(vector * vector)))
    return np.stack(columns, 1)


def fit_tables():
    table = poly_table(F, P_SIZE)
    out = np.zeros((4, 128, 48), np.float32)
    for me in range(4):
        for c in range(8):
            for k2 in range(2):
                row = 8 * c + 4 * k2
                for term in range(P_SIZE):
                    column = 16 * term + 2 * c + k2
                    out[me, row : row + 4, column] = table[4 * me : 4 * me + 4, term]
                    out[me, 64 + row : 68 + row, column] = table[4 * me : 4 * me + 4, term]
    return out


def mat_mul(a, b):
    re, im = [], []
    for r in range(2):
        for c in range(2):
            x, y, u, v = a[2 * r], a[4 + 2 * r], b[c], b[4 + c]
            x1, y1, u1, v1 = a[2 * r + 1], a[5 + 2 * r], b[2 + c], b[6 + c]
            re.append((x * u - y * v) + (x1 * u1 - y1 * v1))
            im.append((x * v + y * u) + (x1 * v1 + y1 * u1))
    return re + im


def mat_mul_herm(a, b):
    re, im = [], []
    for r in range(2):
        for c in range(2):
            x, y, u, v = a[2 * r], a[4 + 2 * r], b[2 * c], b[4 + 2 * c]
            x1, y1, u1, v1 = a[2 * r + 1], a[5 + 2 * r], b[2 * c + 1], b[5 + 2 * c]
            re.append((x * u + y * v) + (x1 * u1 + y1 * v1))
            im.append((y * u - x * v) + (y1 * u1 - x1 * v1))
    return re + im


def herm_mat_mul(a, b):
    re, im = [], []
    for r in range(2):
        for c in range(2):
            x, y, u, v = a[r], a[4 + r], b[c], b[4 + c]
            x1, y1, u1, v1 = a[2 + r], a[6 + r], b[2 + c], b[6 + c]
            re.append((x * u + y * v) + (x1 * u1 + y1 * v1))
            im.append((x * v - y * u) + (x1 * v1 - y1 * u1))
    return re + im


def square_right(z):
    d0 = (z[0] * z[0] + z[4] * z[4]) + (z[1] * z[1] + z[5] * z[5])
    d1 = (z[2] * z[2] + z[6] * z[6]) + (z[3] * z[3] + z[7] * z[7])
    re = (z[0] * z[2] + z[4] * z[6]) + (z[1] * z[3] + z[5] * z[7])
    im = (z[4] * z[2] - z[0] * z[6]) + (z[5] * z[3] - z[1] * z[7])
    return [d0, d1, re, im]


def square_left(w):
    d0 = (w[0] * w[0] + w[4] * w[4]) + (w[2] * w[2] + w[6] * w[6])
    d1 = (w[1] * w[1] + w[5] * w[5]) + (w[3] * w[3] + w[7] * w[7])
    re = (w[0] * w[1] + w[4] * w[5]) + (w[2] * w[3] + w[6] * w[7])
    im = (w[0] * w[5] - w[4] * w[1]) + (w[2] * w[7] - w[6] * w[3])
    return [d0, d1, re, im]


def three_terms(x):
    hi = x.astype(BF16)
    rest = x - hi.astype(F32)
    mid = rest.astype(BF16)
    return hi, mid, (rest - mid.astype(F32)).astype(BF16)


def dot(a, b, dims):
    return lax.dot_general(a, b, (dims, ((), ())), preferred_element_type=F32)


def exact_dot(a, b, dims):
    return lax.dot_general(
        a, b, (dims, ((), ())), precision=lax.Precision.HIGHEST, preferred_element_type=F32
    )


def copies_kernel(line_ref, out_ref):
    for column in range(8):
        out_ref[column] = line_ref[...]


def slot_index(side, rows):
    slot = lax.broadcasted_iota(jnp.int32, (rows, 256), 1)
    return slot // 16 if side == 0 else slot % 16


def start_kernel(gains_hbm, map_hbm, out_ref, gains_ref, map_ref, rows_ref, sem):
    copies = [pltpu.make_async_copy(map_hbm, map_ref, sem.at[4])]
    for n in range(4):
        rows = pl.ds(64 * n, 64)
        copies.append(pltpu.make_async_copy(gains_hbm.at[rows], gains_ref.at[rows], sem.at[n]))
    for copy in copies:
        copy.start()
    rows_ref[...] = jnp.zeros(rows_ref.shape, F32)
    for copy in copies:
        copy.wait()
    rows_ref[:, 0:8] = gains_ref[...]
    parts = []
    for half in range(2):
        tiles = []
        for quad in (2 * half, 2 * half + 1):
            for c in range(8):
                tiles.append(rows_ref[pl.ds(quad * 64 + c, 8, stride=8), :])
        parts.append(jnp.transpose(jnp.concatenate(tiles, 0))[0:8])
    lane = lax.broadcasted_iota(jnp.int32, (1, 128), 1)
    blocks = map_ref[...].astype(F32)
    parts.append(jnp.where(lane == 0, blocks[:, 0:1], blocks[:, 1:2]))
    out_ref[...] = jnp.concatenate(parts * 8, 0)


def spread_kernel(
    coh_ref, vis_ref, weight_ref, plain_ref, masked_ref, observed_ref, expand_ref, reduce_ref, c_ref, v_ref
):
    pick_tables(expand_ref, reduce_ref)
    vis = vis_ref[...].astype(F32)
    for h in range(2):
        at = slice(128 * h, 128 * h + 128)
        c_ref[h] = coh_ref[:, at].astype(F32)
        v_ref[h, 0:64] = vis[:, at]
        v_ref[h, 64:128] = vis[:, at]
        weight = weight_ref[:, at]
        for t in range(2):
            for c in range(8):
                observed_ref[h, t, c] = v_ref[h, pl.ds(t * 8 + c, 8, stride=16), :]
                for quad in range(QUADS):
                    rows = c_ref[h, pl.ds(quad * 128 + t * 8 + c, 8, stride=16), :]
                    plain_ref[h, t, quad, c] = rows
                    masked_ref[h, t, quad, c] = rows * weight


def over_quads(x):
    return x + pltpu.roll(x, 4, 0)


def pick_tables(expand_ref, reduce_ref):
    station = lax.broadcasted_iota(jnp.int32, (STATIONS, 256), 0)
    picks = []
    for side in range(2):
        pick = (station - 16 * side == slot_index(side, STATIONS)).astype(F32)
        inside = (station >= 16 * side) & (station < 16 * side + 16)
        picks.append(jnp.where(inside, pick, 0.0))
    pick = jnp.concatenate(picks, 1)
    rest = jnp.zeros((128 - 3 * STATIONS, 512), F32)
    expand_ref[...] = jnp.concatenate([pick] * 3 + [rest], 0).astype(BF16)
    row = lax.broadcasted_iota(jnp.int32, (16, 256), 0)
    rows = [(row == slot_index(side, 16)).astype(F32) for side in range(2)]
    reduce_ref[...] = jnp.concatenate(rows, 0).astype(BF16)


def expand_gains(gains, pick_ref, pair_ref):
    rest = jnp.zeros((256, 128 - 3 * STATIONS), F32)
    terms = [term.astype(F32) for term in three_terms(gains)]
    pair_ref[...] = dot(
        jnp.concatenate(terms + [rest], 1).astype(BF16), pick_ref[...], ((1,), (0,))
    )


def coefficients(gains, tables_ref, coef_ref):
    coef_ref[...] = jnp.concatenate(
        [
            exact_dot(gains[64 * quad : 64 * quad + 64], tables_ref[0:64], ((0,), (0,)))
            for quad in range(QUADS)
        ],
        1,
    )


def tile_terms(c_ref, v_ref, pick_ref, msg_ref, pair_ref, z_ref, s_ref):
    def half_step(h):
        lanes = slice(128 * h, 128 * h + 128)
        lanes_q = slice(128 * h + 256, 128 * h + 384)
        for t in range(2):
            total = None
            for quad in range(QUADS):
                cs = [c_ref[h, t, quad, c] for c in range(8)]
                rows = [slice(64 * quad + 8 * c, 64 * quad + 8 * c + 8) for c in range(8)]
                gp = [pair_ref[r, lanes] for r in rows]
                gq = [pair_ref[r, lanes_q] for r in rows]
                z = mat_mul_herm(cs, gq)
                for c in range(8):
                    z_ref[quad, c] = z[c]
                m = mat_mul(gp, z)
                total = m if total is None else [x + y for x, y in zip(total, m)]
            resid = [
                v_ref[h, t, c] - over_quads(total[c])
                for c in range(8)
            ]
            for quad in range(QUADS):
                z = [z_ref[quad, c] for c in range(8)]
                terms_p = mat_mul_herm(resid, z) + square_right(z)
                cs = [c_ref[h, t, quad, c] for c in range(8)]
                gp = [pair_ref[64 * quad + 8 * c : 64 * quad + 8 * c + 8, lanes] for c in range(8)]
                w = mat_mul(gp, cs)
                terms_q = herm_mat_mul(resid, w) + square_left(w)
                for side, terms in ((0, terms_p), (1, terms_q)):
                    for c in range(12):
                        rows = slice(96 * quad + 8 * c, 96 * quad + 8 * c + 8)
                        if t == 0:
                            s_ref[side, rows, lanes] = terms[c]
                        else:
                            s_ref[side, rows, lanes] += terms[c]
    for h in range(2):
        half_step(h)
    def sums(side, first, count):
        terms = s_ref[side, first : first + count]
        hi = terms.astype(BF16)
        lo = (terms - hi.astype(F32)).astype(BF16)
        pick = pick_ref[16 * side : 16 * side + 16]
        return dot(pick, lo, ((1,), (1,))) + dot(pick, hi, ((1,), (1,)))

    for half in range(2):
        first = 192 * half
        rest = [sums(side, first + 128, 64) for side in range(2)]
        parts = [sums(0, first, 128), sums(1, first, 128), jnp.concatenate(rest, 1)]
        for n, part in enumerate(parts):
            for z in range(8):
                msg_ref[8 * half + z, 16 * n : 16 * n + 16] = part


def first_tile_kernel(
    c_ref, v_ref, expand_ref, reduce_ref, gall_ref, tables_ref, msg_ref, gains_ref, coef_ref,
    pair_ref, z_ref, s_ref,
):
    pair = lax.axis_index("pairs")
    tile = gall_ref[pl.ds(17 * pair + 16, 1), :].astype(jnp.int32)
    a, b = 34 * tile[0, 0], 34 * tile[0, 1]
    starts = [a, a + 17, b, b + 17, 17 * pair]
    turned = []
    for half in range(2):
        rows = [gall_ref[pl.ds(start + 8 * half, 8), :] for start in starts]
        turned.append(jnp.transpose(jnp.concatenate(rows, 0)))
    gains = jnp.concatenate(turned, 0)
    gains_ref[...] = gains
    expand_gains(gains, expand_ref, pair_ref)
    tile_terms(c_ref, v_ref, reduce_ref, msg_ref, pair_ref, z_ref, s_ref)
    coefficients(gains_ref[...], tables_ref, coef_ref)


def share_kernel(got_ref, plan_ref, out_ref, table_ref):
    level = lax.axis_index("pairs") % 8
    half = pl.multiple_of(8 * (level % 2), 8)
    blocks = [[plan_ref[n, side] for side in range(2)] for n in range(24)]
    table_ref[...] = jnp.zeros(table_ref.shape, F32)
    for n in range(16):
        rest = got_ref[n, 32:48]
        table_ref[blocks[n][0], 0:16] += got_ref[n, 0:16]
        table_ref[blocks[n][0], 16:32] += rest
        table_ref[blocks[n][1], 0:16] += got_ref[n, 16:32]
        table_ref[blocks[n][1], 16:32] += pltpu.roll(rest, 64, 1)
    lane = lax.broadcasted_iota(jnp.int32, (16, 128), 1)
    for target in range(8):
        a, b = blocks[16 + target]
        own = 4 * target + level // 2
        out_ref[target, 0:16] = table_ref[a, 0:16]
        out_ref[target, 16:32] = table_ref[b, 0:16]
        out_ref[target, 32:48] = jnp.where(
            lane < 64, table_ref[a, 16:32], pltpu.roll(table_ref[b, 16:32], 64, 1)
        )
        out_ref[target, 48:56] = table_ref[own, pl.ds(half, 8), :]
        out_ref[target, 56:64] = table_ref[own, pl.ds(16 + half, 8), :]


def update_gains(got_ref, gains_ref, coefs, tables_ref, pen_ref):
    turned = []
    for half in range(2):
        sums = got_ref[4 * half]
        for n in range(1, 4):
            sums = sums + got_ref[4 * half + n]
        rest = sums[32:48]
        first = jnp.concatenate([sums[0:32], sums[48:56]], 0)
        rest = jnp.concatenate([rest, pltpu.roll(rest, 64, 1), sums[56:64]], 0)
        turned += [jnp.transpose(first), jnp.transpose(rest)[0:64]]
    normal = jnp.concatenate(turned, 0)
    coef = coefs[0][...] + coefs[1][...]
    new = []
    for quad in range(QUADS):
        consensus = exact_dot(
            tables_ref[64:128], coef[:, 48 * quad : 48 * quad + 48], ((1,), (1,))
        )
        penalty = pen_ref[8 * quad : 8 * quad + 8, 0:STATIONS]
        g = [gains_ref[64 * quad + 8 * c : 64 * quad + 8 * c + 8] for c in range(8)]
        n = [normal[96 * quad + 8 * c : 96 * quad + 8 * c + 8] for c in range(12)]
        u = [n[c] + penalty * (consensus[8 * c : 8 * c + 8] - g[c]) for c in range(8)]
        h0, h1, off_re, off_im = n[8] + penalty, n[9] + penalty, n[10], n[11]
        scale = 1.0 / (h0 * h1 - off_re * off_re - off_im * off_im)
        new_re, new_im = [], []
        for r in range(2):
            x, y, x1, y1 = u[2 * r], u[4 + 2 * r], u[2 * r + 1], u[5 + 2 * r]
            new_re.append(g[2 * r] + (x * h1 - (x1 * off_re + y1 * off_im)) * scale)
            new_re.append(g[2 * r + 1] + (x1 * h0 - (x * off_re - y * off_im)) * scale)
            new_im.append(g[4 + 2 * r] + (y * h1 - (y1 * off_re - x1 * off_im)) * scale)
            new_im.append(g[5 + 2 * r] + (y1 * h0 - (y * off_re + x * off_im)) * scale)
        new += new_re + new_im
    return jnp.concatenate(new, 0)


def tile_kernel(
    c_ref, v_ref, expand_ref, reduce_ref, pen_ref, got_ref, gains_ref, near_ref, far_ref, tables_ref,
    msg_ref, new_ref, coef_ref, pair_ref, z_ref, s_ref,
):
    gains = update_gains(got_ref, gains_ref, (near_ref, far_ref), tables_ref, pen_ref)
    new_ref[...] = gains
    expand_gains(gains, expand_ref, pair_ref)
    tile_terms(c_ref, v_ref, reduce_ref, msg_ref, pair_ref, z_ref, s_ref)
    coefficients(new_ref[...], tables_ref, coef_ref)


def last_kernel(
    c_ref, v_ref, expand_ref, pen_ref, got_ref, gains_ref, near_ref, far_ref, tables_ref,
    solved_ref, resid_ref, pair_ref, turn_ref, r_ref,
):
    gains = update_gains(got_ref, gains_ref, (near_ref, far_ref), tables_ref, pen_ref)
    turn_ref[:, 0:STATIONS] = gains
    for quad in range(QUADS):
        for k2 in range(2):
            for f in range(4):
                rows = turn_ref[pl.ds(64 * quad + 4 * k2 + f, 8, stride=8), :]
                solved_ref[2 * quad + k2, f] = rows[:, 32:40]
    expand_gains(gains, expand_ref, pair_ref)

    def half_step(h):
        lanes = slice(128 * h, 128 * h + 128)
        lanes_q = slice(128 * h + 256, 128 * h + 384)
        for t in range(2):
            total = None
            for quad in range(QUADS):
                cs = [c_ref[h, t, quad, c] for c in range(8)]
                rows = [slice(64 * quad + 8 * c, 64 * quad + 8 * c + 8) for c in range(8)]
                m = mat_mul(
                    [pair_ref[r, lanes] for r in rows],
                    mat_mul_herm(cs, [pair_ref[r, lanes_q] for r in rows]),
                )
                total = m if total is None else [x + y for x, y in zip(total, m)]
            for c in range(8):
                observed = v_ref[h, t, c]
                r_ref[h, pl.ds(t * 8 + c, 8, stride=16), :] = observed - over_quads(total[c])
    for h in range(2):
        half_step(h)
    for h in range(2):
        resid_ref[:, 128 * h : 128 * h + 128] = r_ref[h, 0:64].astype(BF16)


VMEM = pl.BlockSpec(memory_space=pltpu.VMEM)
SMEM = pl.BlockSpec(memory_space=pltpu.SMEM)


def call(kernel, in_specs, out_shapes, scratch, flops, limit=24):
    return pl.pallas_call(
        kernel,
        in_specs=in_specs,
        out_specs=[VMEM] * len(out_shapes),
        out_shape=[jax.ShapeDtypeStruct(s, d) for s, d in out_shapes],
        scratch_shapes=[pltpu.VMEM(*s) if isinstance(s, tuple) else s for s in scratch],
        compiler_params=pltpu.CompilerParams(vmem_limit_bytes=limit * 1024 * 1024),
        cost_estimate=pl.CostEstimate(flops=flops, bytes_accessed=1 << 19, transcendentals=0),
    )


WORK = [((256, 512), F32)]
TERMS = [((QUADS, 8, 8, 128), F32), ((2, 384, 256), F32)]
TILE_OUT = [((16, 48, 128), F32), ((256, STATIONS), F32), ((STATIONS, 192), F32)]
ALONG_Z = [[8 * column + z for z in range(8)] for column in range(8)]
ALONG_XZ = [[32 * x + 8 * y + z for x in range(2) for z in range(8)] for y in range(4)]
ACROSS = [[8 * column + z for column in range(8)] for z in range(8)]


def exchange(x, groups=None):
    return lax.all_to_all(x, "pairs", 0, 0, tiled=True, axis_index_groups=groups)


def local(coherency, visibility, tile_map, flag_mask, gains_start, penalty):
    pair = lax.axis_index("pairs")
    chan = lax.axis_index("chan")
    tables = lax.dynamic_index_in_dim(jnp.asarray(fit_tables()), chan, 0, keepdims=False)
    coh = coherency.reshape(512, 256)
    vis = visibility.reshape(64, 256)
    weight = flag_mask.astype(F32)

    def from_chan(x, d):
        return lax.ppermute(x, "chan", [(i, i ^ d) for i in range(4)])

    (spread,) = call(
        start_kernel,
        [pl.BlockSpec(memory_space=pl.ANY)] * 2,
        [((8 * 17, 128), F32)],
        [((256, 8), F32), ((1, 2), jnp.int32), ((256, 128), F32), pltpu.SemaphoreType.DMA((5,))],
        1 << 17,
        60,
    )(gains_start.reshape(256, 8), tile_map)
    line = exchange(spread.reshape(8, 17, 1, 128), ALONG_Z).reshape(136, 128)
    (lines,) = call(copies_kernel, [VMEM], [((8, 136, 128), F32)], [], 1 << 16)(line)
    gall = exchange(lines, ACROSS).reshape(64 * 17, 128)
    penalty = jnp.broadcast_to(jnp.repeat(penalty, 4)[:, None], (32, 128))
    plain, masked, observed, expand, reduce = call(
        spread_kernel,
        [VMEM] * 3,
        [((2, 2, QUADS, 8, 8, 128), F32)] * 2
        + [((2, 2, 8, 8, 128), F32), ((128, 512), BF16), ((32, 256), BF16)],
        [((2, 512, 128), F32), ((2, 128, 128), F32)],
        1 << 20,
    )(coh, vis, weight)
    gall, tables, penalty, plain, masked, observed, expand, reduce = lax.optimization_barrier(
        (gall, tables, penalty, plain, masked, observed, expand, reduce)
    )
    maps = gall.reshape(8, 8, 17, 128)[:, :, 16, 0:2].astype(jnp.int32)
    plan = jnp.concatenate(
        [
            lax.dynamic_index_in_dim(
                maps.reshape(2, 4, 8, 2), pair // 8 % 4, 1, keepdims=False
            ).reshape(16, 2),
            lax.dynamic_index_in_dim(maps, pair % 8, 1, keepdims=False),
        ],
        0,
    )
    msg, gains, coef = call(
        first_tile_kernel,
        [VMEM] * 6,
        TILE_OUT,
        WORK + TERMS,
        8 << 20,
    )(masked, observed, expand, reduce, gall, tables)
    for sweep in range(ITERS):
        got = exchange(msg, ALONG_XZ)
        near = coef + from_chan(coef, 1)
        coefs = [near, from_chan(near, 2)]
        got, plan, *coefs = lax.optimization_barrier((got, plan, *coefs))
        (share,) = call(
            share_kernel, [VMEM, VMEM], [((8, 64, 128), F32)], [((BLOCKS, 32, 128), F32)], 1 << 20
        )(got, plan)
        sums = exchange(share, ACROSS)
        if sweep + 1 < ITERS:
            msg, gains, coef = call(
                tile_kernel,
                [VMEM] * 10,
                TILE_OUT,
                WORK + TERMS,
                8 << 20,
            )(masked, observed, expand, reduce, penalty, sums, gains, *coefs, tables)
    solved, residual = call(
        last_kernel,
        [VMEM] * 9,
        [((K, 4, 8, 8), F32), ((64, 256), BF16)],
        WORK + [((256, 128), F32), ((2, 128, 128), F32)],
        4 << 20,
    )(plain, observed, expand, penalty, sums, gains, *coefs, tables)
    return (solved, residual.reshape(visibility.shape))


def solution(mesh):
    in_specs = (
        P("pairs", None, "chan", None, None, None),
        P("pairs", "chan", None, None, None),
        P("pairs", None),
        P("pairs", None),
        P(None, "chan", None, "pairs"),
        P(),
    )
    out_specs = (P(None, "chan", None, "pairs"), P("pairs", "chan", None, None, None))
    return jax.shard_map(local, mesh=mesh, in_specs=in_specs, out_specs=out_specs, check_vma=False)
```
